512 devices in a mesh: dp: 64 (over z, x, core), tensor: 8 (over y).
Axes of the slice: x: 4, y: 8, z: 8, core: 2. Of those that a mesh axis runs over, the one named last changes fastest.
Arguments:
- head_inputs: bfloat16 [64, 3, 1025, 2048], P('dp', None, None, 'tensor'), may hold values from -6 to 6
- out_weight: bfloat16 [3200, 2048], P('dp', 'tensor'), may hold values from -0.109375 to 0.109375
- sequence_gradient: bfloat16 [4, 32768, 3200], P(None, 'dp', 'tensor'), may hold values from -16 to 16
- slot_labels: int32 [64, 32], P('dp'), may hold values from -1 to 1023, as said below
Outputs:
- head_gradient: bfloat16 [64, 3, 1025, 2048], P('dp', None, None, 'tensor')
- weight_gradient: float32 [3200, 2048], P('dp', 'tensor')
The draws below stay inside these ranges and needn't reach their ends.
Inputs may be any that keep to these rules, and one draw needn't show every extreme that they name: `slot_labels`: entry (g, s) labels slot s of shard g: -1 where the slot holds no tile's piece, else t * 16 + i for piece i of tile t. Each of the 1024 pieces appears exactly once; the 16 pieces of one tile lie in 16 different shards; a shard holds at most 32 pieces, and some shard holds exactly 32.
All inputs are finite; a program needn't handle non-finite values.
Results may differ from the reference program's by a relative error of at most 0.019.
Values may be sent and summed in bfloat16 or wider, within the bound.
No kernel may reach another device: no remote copies, remote signals or barrier semaphores. Data moves between devices by JAX's collectives and lax.ppermute only.
A program may use at most 128 MiB of HBM per device.

```python
import math
import jax
import jax.numpy as jnp
from jax import lax

D = 3200
HD = 128
GRID = 32
PIECE = 16
HALL = 2048
TT = 1025
SHUF = 256
NPIECE = 16
SLOTS = 32
MOST = 32
TILES = 64
LM_TOTAL = 32768


def draw_head_inputs(key, part):
    key = jax.random.fold_in(key, 11)
    shape = (TILES, 3, TT, HALL)
    base = 1.5 * jax.random.truncated_normal(key, -4.0, 4.0, shape, jnp.float32)
    return base.astype(jnp.bfloat16)


def draw_slot_labels(key, part):
    key = jax.random.fold_in(key, 7)
    keys = jax.random.split(key, 4)
    shards = TILES
    half_count = shards // 2
    spread = jax.random.randint(keys[0], (half_count,), 0, MOST - NPIECE + 1)
    spread = spread.at[0].set(MOST - NPIECE)
    loads = jnp.stack([NPIECE + spread, NPIECE - spread], axis=1).reshape(shards)
    loads = loads[jax.random.permutation(keys[1], shards)]
    ends = jnp.cumsum(loads)
    starts = ends - loads
    positions = jnp.arange(NPIECE * shards, dtype=jnp.int32)
    holder = jnp.sum((ends[None, :] <= positions[:, None]).astype(jnp.int32), axis=1)
    rank = positions - starts[holder]
    piece_index = positions // shards
    tile_index = jax.random.permutation(keys[2], shards)[positions % shards]
    slot_orders = jax.vmap(lambda one_key: jax.random.permutation(one_key, SLOTS))(jax.random.split(keys[3], shards))
    slot_index = slot_orders[holder, rank]
    labels = jnp.full((shards, SLOTS), -1, jnp.int32)
    labels = labels.at[holder, slot_index].set((tile_index * NPIECE + piece_index).astype(jnp.int32))
    return labels


def with_spikes(result, own_key, source, target, shards_of, factor):
    def block_of(axis_at):
        return (jnp.arange(result.shape[axis_at]) // (result.shape[axis_at] // shards_of)).reshape((-1,) + (1,) * (result.ndim - 1 - axis_at))

    one_side = jax.random.permutation(own_key, shards_of)[block_of(target)]
    other_side = (block_of(target) + shards_of // 2) % shards_of
    return jnp.where((block_of(source) == one_side) | (block_of(source) == other_side), factor * result, result)


def shard_levels(stream_key, dims, cuts, least, top_value):
    gain, own = 1.0, jax.random.fold_in(stream_key, 6)
    for position, blocks in cuts:
        draws = jnp.exp(jax.random.uniform(jax.random.fold_in(own, position), (blocks,), jnp.float32, least / len(cuts), top_value / len(cuts)))
        gain = gain * jnp.repeat(draws, dims[position] // blocks).reshape([-1 if axis == position else 1 for axis in range(len(dims))])
    return gain


def noise(rng, shape, scale, limit, cuts=(), kind=jnp.bfloat16):
    drawn = scale * jax.random.normal(rng, shape, jnp.float32)
    if cuts:
        drawn = drawn * shard_levels(rng, shape, cuts, -0.22, 0.18)
    return jnp.clip(drawn, -limit, limit).astype(kind)


def bell_draw_with(key, dims, scale, limit, pieces, heavy, kind=jnp.bfloat16):
    values = scale * jax.random.normal(key, dims, jnp.float32)
    if pieces:
        values = values * shard_levels(key, dims, pieces, -0.22, 0.18)
    return jnp.clip(with_spikes(values, jax.random.fold_in(key, 3), *heavy), -limit, limit).astype(kind)


def setup_inputs(seed: int = 0) -> dict:
    seeds = jax.random.split(jax.random.key(seed), 5)
    head_inputs = draw_head_inputs(jax.random.fold_in(seeds[4], 71), 0)
    out_weight = noise(seeds[1], (D, HALL), D ** -0.5, 0.109375, ((0, 64), (1, 8)))
    sequence_gradient = bell_draw_with(seeds[2], (4, LM_TOTAL, D), 1.0, 16.0, ((1, 64), (2, 8)), (1, 2, 64, 4.0))
    slot_labels = draw_slot_labels(jax.random.fold_in(seeds[4], 71), 0)
    return {"head_inputs": head_inputs, "out_weight": out_weight, "sequence_gradient": sequence_gradient, "slot_labels": slot_labels}


def shuffle_order(patch_rows):
    half_grid = GRID // 2
    width = patch_rows.shape[-1]
    phased = patch_rows.reshape(half_grid, 2, half_grid, 2, width).transpose(1, 3, 0, 2, 4)
    return phased.reshape(4, SHUF, width)

def patch_order(shuffled):
    half_grid = GRID // 2
    width = shuffled.shape[-1]
    phased = shuffled.reshape(2, 2, half_grid, half_grid, width).transpose(2, 0, 3, 1, 4)
    return phased.reshape(GRID * GRID, width)

def split_heads(token_rows):
    return token_rows.reshape(TT, HALL // HD, HD).transpose(1, 0, 2)

def head_pass(query_rows, key_rows, value_rows, out_grad):
    score_scale = HD ** (-0.5)
    scores = jnp.dot(query_rows, key_rows.T, preferred_element_type=jnp.float32) * score_scale
    shifted = jnp.exp(scores - lax.optimization_barrier(jnp.max(scores, axis=1, keepdims=True)))
    probs = shifted / lax.optimization_barrier(jnp.sum(shifted, axis=1, keepdims=True))
    probs_low = probs.astype(jnp.bfloat16)
    attended = jnp.dot(probs_low, value_rows, preferred_element_type=jnp.float32).astype(jnp.bfloat16)
    prob_grad = jnp.dot(out_grad, value_rows.T, preferred_element_type=jnp.float32)
    row_delta = lax.optimization_barrier(jnp.sum(out_grad.astype(jnp.float32) * attended.astype(jnp.float32), axis=1, keepdims=True))
    score_grad = (probs * (prob_grad - row_delta)).astype(jnp.bfloat16)
    query_grad = (jnp.dot(score_grad, key_rows, preferred_element_type=jnp.float32) * score_scale).astype(jnp.bfloat16)
    key_grad = (jnp.dot(score_grad.T, query_rows, preferred_element_type=jnp.float32) * score_scale).astype(jnp.bfloat16)
    value_grad = jnp.dot(probs_low.T, out_grad, preferred_element_type=jnp.float32).astype(jnp.bfloat16)
    return (attended, jnp.stack([query_grad, key_grad, value_grad]))

def reference(head_inputs, out_weight, sequence_gradient, slot_labels):
    total_slots = slot_labels.shape[0] * slot_labels.shape[1]
    flat_labels = slot_labels.reshape(total_slots)
    dump_index = TILES * NPIECE
    targets = jnp.where(flat_labels >= 0, flat_labels, dump_index).astype(jnp.int32)
    source_slot = jnp.zeros((dump_index + 1,), jnp.int32).at[targets].set(jnp.arange(total_slots, dtype=jnp.int32))
    source_slot = source_slot[:dump_index].reshape(TILES, NPIECE)
    slot_view = sequence_gradient.reshape(4, total_slots, PIECE, D)
    weight_wide = out_weight.astype(jnp.float32)

    def tile_step(weight_total, tile_inputs):
        inputs_tile, slot_ids = tile_inputs
        returned = slot_view[:, slot_ids].reshape(4, SHUF, D)
        returned_wide = returned.astype(jnp.float32)
        grad_shuffled = jnp.einsum('krf,fh->krh', returned_wide, weight_wide, precision=lax.Precision.HIGHEST)
        grad_shuffled = grad_shuffled.astype(jnp.bfloat16)
        out_grad = jnp.concatenate([jnp.zeros((1, HALL), jnp.bfloat16), patch_order(grad_shuffled)], axis=0)
        heads_in = (split_heads(inputs_tile[0]), split_heads(inputs_tile[1]), split_heads(inputs_tile[2]), split_heads(out_grad))
        attended, grads = lax.map(lambda group: head_pass(*group), heads_in)
        attended_rows = attended.transpose(1, 0, 2).reshape(TT, HALL)
        shuffled_out = shuffle_order(attended_rows[1:]).astype(jnp.float32)
        weight_total = weight_total + jnp.einsum('krf,krh->fh', returned_wide, shuffled_out, precision=lax.Precision.HIGHEST)
        tile_grad = grads.transpose(1, 2, 0, 3).reshape(3, TT, HALL)
        return (weight_total, tile_grad)
    weight_total, head_gradient = lax.scan(tile_step, jnp.zeros((D, HALL), jnp.float32), (head_inputs, source_slot))
    weight_gradient = weight_total * (1.0 / math.sqrt(TILES * GRID * GRID))
    return (head_gradient, weight_gradient)
```

```python
import functools
import math

import jax
import jax.numpy as jnp
from jax import lax
from jax.experimental import pallas as pl
from jax.experimental.pallas import tpu as pltpu
from jax.sharding import Mesh, PartitionSpec as P

HD = 128
TT = 1025
PATCHES = 1024
KPAD = 1040
QPAD = 1152
QBLK = 384
PIECE = 16
NPIECE = 16
MAIN = 384
GROUP = 50
GPAD = 64
BF = jnp.bfloat16
F32 = jnp.float32
SHARDS = ("z", "x", "c")
SCALE = HD ** (-0.5)


def dot(left, right):
    return jnp.dot(left, right, preferred_element_type=F32)


def dot_last(left, right):
    return lax.dot_general(left, right, (((1,), (1,)), ((), ())), preferred_element_type=F32)


def dot_first(left, right):
    return lax.dot_general(left, right, (((0,), (0,)), ((), ())), preferred_element_type=F32)


def iota(shape, axis):
    return lax.broadcasted_iota(jnp.int32, shape, axis)


def params():
    return pltpu.CompilerParams(vmem_limit_bytes=50 * 1024 * 1024)


def pack_kernel(label_ref, rows_ref, out0_ref, out1_ref, rest_ref):
    slots = label_ref.shape[1]
    rest = jnp.zeros(rest_ref.shape, F32)
    for k in range(4):
        place = (iota((16, 128), 1) == iota((16, 128), 0) + 16 * k).astype(F32).astype(BF)
        rest = rest + dot(rows_ref[k, :, MAIN : MAIN + 16], place)
    rest_ref[...] = rest
    lane = iota((PIECE, 128), 1)
    nothing = jnp.where(lane == 64, -1.0, 0.0).astype(BF)

    def clear(d, carry):
        out0_ref[d, :, 2 * MAIN :] = nothing
        return carry

    lax.fori_loop(0, out0_ref.shape[0], clear, 0)

    def place_slot(s, carry):
        label = label_ref[0, s]

        @pl.when(label >= 0)
        def _():
            owner = label >> 4
            piece = label & 15
            rows = pl.ds(pl.multiple_of(s * PIECE, PIECE), PIECE)
            out0_ref[owner, :, 0:MAIN] = rows_ref[0, rows, 0:MAIN]
            out0_ref[owner, :, MAIN : 2 * MAIN] = rows_ref[1, rows, 0:MAIN]
            out1_ref[owner, :, 0:MAIN] = rows_ref[2, rows, 0:MAIN]
            out1_ref[owner, :, MAIN : 2 * MAIN] = rows_ref[3, rows, 0:MAIN]
            number = piece.astype(F32)
            out0_ref[owner, :, 2 * MAIN :] = jnp.where(lane == 64, number, rest_ref[rows, :]).astype(BF)

        return carry

    lax.fori_loop(0, slots, place_slot, 0)


def pack(labels, rows, peers):
    return pl.pallas_call(
        pack_kernel,
        out_shape=(
            jax.ShapeDtypeStruct((peers, PIECE, 2 * MAIN + 128), BF),
            jax.ShapeDtypeStruct((peers, PIECE, 2 * MAIN), BF),
        ),
        in_specs=[
            pl.BlockSpec(memory_space=pltpu.SMEM),
            pl.BlockSpec(memory_space=pltpu.VMEM),
        ],
        out_specs=(
            pl.BlockSpec(memory_space=pltpu.VMEM),
            pl.BlockSpec(memory_space=pltpu.VMEM),
        ),
        scratch_shapes=[pltpu.VMEM((rows.shape[1], 128), F32)],
        compiler_params=params(),
        name="pack_pieces",
    )(labels, rows)


def receive_kernel(chunk, source_ref, in_ref, rest_in_ref, weight_ref, rows_ref, part_ref, rest_ref, left_scr, stack_scr):
    if chunk == 0:
        for i in range(NPIECE):
            rest_ref[16 * i : 16 * i + 16, :] = in_ref[source_ref[i], :, 2 * MAIN :]
        rest = rest_ref[...]
    else:
        rest = rest_in_ref[...]
    column = iota((MAIN, 8 * GPAD), 1)
    inside = (column & 63) < GROUP
    feature = (column >> 6) * GROUP + (column & 63)
    spread = jnp.where((feature == iota((MAIN, 8 * GPAD), 0)) & inside, 1.0, 0.0).astype(BF)
    for u in range(2):
        for i in range(NPIECE):
            left_scr[16 * i : 16 * i + 16, :] = in_ref[source_ref[i], :, u * MAIN : (u + 1) * MAIN]
        k = 2 * chunk + u
        lane = iota((128, 8 * GPAD), 0)
        spread_rest = jnp.where(
            (feature[0:128] == lane + (MAIN - 16 * k)) & inside[0:128] & (lane >= 16 * k) & (lane < 16 * k + 16),
            1.0,
            0.0,
        ).astype(BF)
        wide = (dot(left_scr[...], spread) + dot(rest, spread_rest)).astype(BF)
        stack_scr[0, u * 128 : (u + 1) * 128, :] = wide[0:128]
        stack_scr[1, u * 128 : (u + 1) * 128, :] = wide[128:256]
    row = iota((256, 256), 0)
    wanted = (row & 1) * 128 + (row >> 5) * 16 + ((row >> 1) & 15)
    order = jnp.where(iota((256, 256), 1) == wanted, 1.0, 0.0).astype(BF)
    for half in range(2):
        rows_ref[half * 256 : (half + 1) * 256, :] = dot(order, stack_scr[half]).astype(BF)
    rows = rows_ref[...]
    for a in range(8):
        part_ref[a] = dot(rows, weight_ref[:, a * 256 : (a + 1) * 256]).astype(BF)


def receive(chunk, source, arrived, rest, weight):
    vmem = pl.BlockSpec(memory_space=pltpu.VMEM)
    return pl.pallas_call(
        functools.partial(receive_kernel, chunk),
        out_shape=(
            jax.ShapeDtypeStruct((512, 512), BF),
            jax.ShapeDtypeStruct((8, 512, 256), BF),
            jax.ShapeDtypeStruct((256, 128), BF),
        ),
        in_specs=[pl.BlockSpec(memory_space=pltpu.SMEM), vmem, vmem, vmem],
        out_specs=(vmem, vmem, vmem),
        scratch_shapes=[pltpu.VMEM((256, MAIN), BF), pltpu.VMEM((2, 256, 512), BF)],
        compiler_params=params(),
        name=f"receive_{chunk}",
    )(source, arrived, rest, weight)


def forward_kernel(x_ref, p_ref, att_ref, a_ref, q_scr, vt_scr, a_scr):
    tail_row = iota((16, 128), 0) == 0
    q_scr[0:1024, :] = x_ref[0, 0, 0:1024, :]
    q_scr[1024:QPAD, :] = jnp.zeros((128, 128), BF)
    q_scr[1024:1040, :] = jnp.where(tail_row, x_ref[0, 0, 1024:1025, :].astype(F32), 0.0).astype(BF)
    key = x_ref[0, 1, 0:1024, :]
    key_tail = jnp.where(tail_row, x_ref[0, 1, 1024:1025, :].astype(F32), 0.0).astype(BF)
    vt_scr[...] = x_ref[0, 2, 0:1024, :].astype(F32).T.astype(BF)
    value_tail = jnp.where(tail_row, x_ref[0, 2, 1024:1025, :].astype(F32), 0.0).astype(BF)
    first = iota((16, QBLK), 0) == 0
    for j in range(QPAD // QBLK):
        span = slice(j * QBLK, (j + 1) * QBLK)
        query = q_scr[span, :]
        score = dot_last(key, query) * SCALE
        score_tail = (dot_last(key_tail, query) * SCALE)[0:1]
        top = jnp.maximum(jnp.max(score, axis=0, keepdims=True), score_tail)
        shifted = jnp.exp(score - top)
        shifted_tail = jnp.exp(score_tail - top)
        inverse = 1.0 / (jnp.sum(shifted, axis=0, keepdims=True) + shifted_tail)
        low = (shifted * inverse).astype(BF)
        low_tail = jnp.where(first, shifted_tail * inverse, 0.0).astype(BF)
        p_ref[0, 0:1024, span] = low
        p_ref[0, 1024:KPAD, span] = low_tail
        att = (dot(vt_scr[...], low) + dot_first(value_tail, low_tail)).T.astype(BF)
        att_ref[span, :] = att
        a_scr[span, :] = att.astype(F32)
    moved = a_scr[pl.ds(1, 1024), :].astype(BF)
    for i in range(NPIECE):
        for e in range(2):
            a_ref[e, 32 * i : 32 * i + 32, :] = moved[64 * i + 32 * e : 64 * i + 32 * e + 32]


def forward(head_inputs):
    return pl.pallas_call(
        forward_kernel,
        grid=(2,),
        out_shape=(
            jax.ShapeDtypeStruct((2, KPAD, QPAD), BF),
            jax.ShapeDtypeStruct((QPAD, 256), BF),
            jax.ShapeDtypeStruct((2, 512, 256), BF),
        ),
        in_specs=[pl.BlockSpec((1, 3, TT, HD), lambda h: (0, 0, 0, h))],
        out_specs=(
            pl.BlockSpec((1, KPAD, QPAD), lambda h: (h, 0, 0)),
            pl.BlockSpec((QPAD, HD), lambda h: (0, h)),
            pl.BlockSpec((2, 512, HD), lambda h: (0, 0, h)),
        ),
        scratch_shapes=[
            pltpu.VMEM((QPAD, HD), BF),
            pltpu.VMEM((HD, 1024), BF),
            pltpu.VMEM((QPAD, HD), F32),
        ],
        compiler_params=params(),
        cost_estimate=pl.CostEstimate(flops=12 * 10**9, bytes_accessed=8 * 10**6, transcendentals=2 * 10**6),
        name="attend",
    )(head_inputs)


def backward_kernel(x_ref, p_ref, att_ref, o0_ref, o1_ref, out_ref, q_scr, kt_scr, g_scr, dq_scr, dk_scr, dv_scr, dkt_scr, dvt_scr):
    tail_row = iota((16, 128), 0) == 0
    q_scr[0:1024, :] = x_ref[0, 0, 0:1024, :]
    q_scr[1024:QPAD, :] = jnp.zeros((128, 128), BF)
    q_scr[1024:1040, :] = jnp.where(tail_row, x_ref[0, 0, 1024:1025, :].astype(F32), 0.0).astype(BF)
    kt_scr[...] = x_ref[0, 1, 0:1024, :].astype(F32).T.astype(BF)
    key_tail = jnp.where(tail_row, x_ref[0, 1, 1024:1025, :].astype(F32), 0.0).astype(BF)
    value = x_ref[0, 2, 0:1024, :]
    value_tail = jnp.where(tail_row, x_ref[0, 2, 1024:1025, :].astype(F32), 0.0).astype(BF)
    g_scr[0:8, :] = jnp.zeros((8, HD), F32)
    g_scr[1024 : QPAD, :] = jnp.zeros((QPAD - 1024, HD), F32)
    for i in range(NPIECE):
        g_scr[pl.ds(1 + 64 * i, 32), :] = o0_ref[32 * i : 32 * i + 32, :].astype(F32)
        g_scr[pl.ds(33 + 64 * i, 32), :] = o1_ref[32 * i : 32 * i + 32, :].astype(F32)
    for j in range(QPAD // QBLK):
        span = slice(j * QBLK, (j + 1) * QBLK)
        query = q_scr[span, :]
        grad_wide = g_scr[span, :]
        grad = grad_wide.astype(BF)
        delta = jnp.sum((grad_wide * att_ref[span, :].astype(F32)).T, axis=0, keepdims=True)
        low = p_ref[0, 0:1024, span]
        low_tail = p_ref[0, 1024:KPAD, span]
        inner = (low.astype(F32) * (dot_last(value, grad) - delta)).astype(BF)
        inner_tail = (low_tail.astype(F32) * (dot_last(value_tail, grad) - delta)).astype(BF)
        dq = (dot(kt_scr[...], inner) + dot_first(key_tail, inner_tail)) * SCALE
        dq_scr[span, :] = dq.T.astype(BF)
        dk, dkt = dot(inner, query), dot(inner_tail, query)
        dv, dvt = dot(low, grad), dot(low_tail, grad)
        if j == 0:
            dk_scr[...], dkt_scr[...], dv_scr[...], dvt_scr[...] = dk, dkt, dv, dvt
        else:
            dk_scr[...] += dk
            dkt_scr[...] += dkt
            dv_scr[...] += dv
            dvt_scr[...] += dvt
    out_ref[0, 0, 0:1024, :] = dq_scr[0:1024, :]
    out_ref[0, 0, 1024:1025, :] = dq_scr[1024:1040, :][0:1]
    out_ref[0, 1, 0:1024, :] = (dk_scr[...] * SCALE).astype(BF)
    out_ref[0, 1, 1024:1025, :] = (dkt_scr[...] * SCALE).astype(BF)[0:1]
    out_ref[0, 2, 0:1024, :] = dv_scr[...].astype(BF)
    out_ref[0, 2, 1024:1025, :] = dvt_scr[...].astype(BF)[0:1]


def backward(head_inputs, probs, att, o0, o1):
    return pl.pallas_call(
        backward_kernel,
        grid=(2,),
        out_shape=jax.ShapeDtypeStruct((1, 3, TT, 256), BF),
        in_specs=[
            pl.BlockSpec((1, 3, TT, HD), lambda h: (0, 0, 0, h)),
            pl.BlockSpec((1, KPAD, QPAD), lambda h: (h, 0, 0)),
            pl.BlockSpec((QPAD, HD), lambda h: (0, h)),
            pl.BlockSpec((512, HD), lambda h: (0, h)),
            pl.BlockSpec((512, HD), lambda h: (0, h)),
        ],
        out_specs=pl.BlockSpec((1, 3, TT, HD), lambda h: (0, 0, 0, h)),
        scratch_shapes=[
            pltpu.VMEM((QPAD, HD), BF),
            pltpu.VMEM((HD, 1024), BF),
            pltpu.VMEM((QPAD, HD), F32),
            pltpu.VMEM((QPAD, HD), BF),
            pltpu.VMEM((1024, HD), F32),
            pltpu.VMEM((1024, HD), F32),
            pltpu.VMEM((16, HD), F32),
            pltpu.VMEM((16, HD), F32),
        ],
        compiler_params=params(),
        name="attend_backward",
    )(head_inputs, probs, att, o0, o1)


def weight_kernel(core_ref, r0_ref, r1_ref, a_ref, keep_ref, send_ref, t0_scr, t1_scr, sum_scr):
    @pl.when(pl.program_id(0) == 0)
    def _():
        t0_scr[...] = r0_ref[...].astype(F32).T.astype(BF)
        t1_scr[...] = r1_ref[...].astype(F32).T.astype(BF)

    sum_scr[...] = dot(t0_scr[...], a_ref[0, 0]) + dot(t1_scr[...], a_ref[0, 1])
    core = core_ref[0]
    for x in range(4):
        mine = pl.multiple_of((2 * x + core) * GPAD, GPAD)
        other = pl.multiple_of((2 * x + 1 - core) * GPAD, GPAD)
        keep_ref[0, x] = sum_scr[pl.ds(mine, GPAD), :][0:GROUP]
        send_ref[0, x] = sum_scr[pl.ds(other, GPAD), :][0:GROUP].astype(BF)


def weight_parts(core, r0, r1, gathered):
    return pl.pallas_call(
        weight_kernel,
        grid=(8,),
        out_shape=(
            jax.ShapeDtypeStruct((8, 4, GROUP, 256), F32),
            jax.ShapeDtypeStruct((8, 4, GROUP, 256), BF),
        ),
        in_specs=[
            pl.BlockSpec(memory_space=pltpu.SMEM),
            pl.BlockSpec((512, 512), lambda a: (0, 0)),
            pl.BlockSpec((512, 512), lambda a: (0, 0)),
            pl.BlockSpec((1, 2, 512, 256), lambda a: (a, 0, 0, 0)),
        ],
        out_specs=(
            pl.BlockSpec((1, 4, GROUP, 256), lambda a: (a, 0, 0, 0)),
            pl.BlockSpec((1, 4, GROUP, 256), lambda a: (a, 0, 0, 0)),
        ),
        scratch_shapes=[
            pltpu.VMEM((512, 512), BF),
            pltpu.VMEM((512, 512), BF),
            pltpu.VMEM((512, 256), F32),
        ],
        compiler_params=params(),
        name="weight_parts",
    )(core, r0, r1, gathered)


def per_device(head_inputs, out_weight, sequence_gradient, slot_labels):
    peers = 64
    swap = [(z * 8 + y, y * 8 + z) for z in range(8) for y in range(8)]
    out0, out1 = pack(slot_labels, sequence_gradient, peers)
    in0 = lax.all_to_all(out0, SHARDS, 0, 0, tiled=True)
    in1 = lax.all_to_all(out1, SHARDS, 0, 0, tiled=True)

    weight = lax.ppermute(out_weight, ("z", "y"), swap)
    weight = lax.all_gather(weight, "z", axis=0)
    weight = lax.all_gather(weight, "x", axis=0)
    weight = lax.all_gather(weight, "c", axis=0)
    weight = jnp.pad(weight, ((0, 0), (0, 0), (0, 0), (0, GPAD - GROUP), (0, 0)))
    weight = weight.transpose(1, 0, 3, 2, 4).reshape(8 * GPAD, 2048)

    probs, att, parts = forward(head_inputs)
    gathered = lax.all_gather(parts, "y", axis=0)

    ids = in0[:, 0, 2 * MAIN + 64].astype(jnp.int32)
    wanted = jnp.arange(NPIECE, dtype=jnp.int32)
    source = jnp.sum(
        jnp.where(ids[None, :] == wanted[:, None], jnp.arange(peers, dtype=jnp.int32)[None, :], 0), axis=1
    )
    r0, part0, rest = receive(0, source, in0, jnp.zeros((256, 128), BF), weight)
    o0 = lax.psum_scatter(part0, "y", scatter_dimension=0, tiled=True)[0]
    r1, part1, _ = receive(1, source, in1, rest, weight)
    o1 = lax.psum_scatter(part1, "y", scatter_dimension=0, tiled=True)[0]

    core = lax.axis_index("c").astype(jnp.int32)[None]
    keep, send = weight_parts(core, r0, r1, gathered)
    got = lax.ppermute(send, "c", [(0, 1), (1, 0)])
    both = (keep + got.astype(F32)).astype(BF).reshape(32, GROUP, 256)
    spread = lax.all_to_all(both, ("z", "x"), 0, 0, tiled=True)
    summed = jnp.sum(spread.astype(F32), axis=0) * (1.0 / math.sqrt(65536))
    weight_gradient = lax.ppermute(summed, ("z", "y"), swap)

    head_gradient = backward(head_inputs, probs, att, o0, o1)
    return head_gradient, weight_gradient


def solution(mesh):
    fine = Mesh(mesh.devices.reshape(8, 4, 2, 8), ("z", "x", "c", "y"))
    return jax.shard_map(
        per_device,
        mesh=fine,
        in_specs=(
            P(SHARDS, None, None, "y"),
            P(SHARDS, "y"),
            P(None, SHARDS, "y"),
            P(SHARDS, None),
        ),
        out_specs=(P(SHARDS, None, None, "y"), P(SHARDS, "y")),
        check_vma=False,
    )
```

```python
import functools
import math

import jax
import jax.numpy as jnp
from jax import lax
from jax.experimental import pallas as pl
from jax.experimental.pallas import tpu as pltpu
from jax.sharding import Mesh, PartitionSpec as P

HD = 128
TT = 1025
PATCHES = 1024
KPAD = 1040
QPAD = 1152
QBLK = 384
PIECE = 16
NPIECE = 16
MAIN = 384
GROUP = 50
GPAD = 64
BF = jnp.bfloat16
F32 = jnp.float32
SHARDS = ("z", "x", "c")
SCALE = HD ** (-0.5)


def dot(left, right):
    return jnp.dot(left, right, preferred_element_type=F32)


def dot_last(left, right):
    return lax.dot_general(left, right, (((1,), (1,)), ((), ())), preferred_element_type=F32)


def dot_first(left, right):
    return lax.dot_general(left, right, (((0,), (0,)), ((), ())), preferred_element_type=F32)


def iota(shape, axis):
    return lax.broadcasted_iota(jnp.int32, shape, axis)


def params():
    return pltpu.CompilerParams(vmem_limit_bytes=50 * 1024 * 1024)


def pack_kernel(label_ref, x_ref, out_ref, rest_scr):
    slots = label_ref.shape[1]
    positions = x_ref.shape[2]
    lane = iota((16, positions), 1)
    slot = lane >> 4
    goal = jnp.full((16, positions), -1, jnp.int32)
    number = jnp.zeros((16, positions), jnp.int32)
    for s in range(slots):
        label = label_ref[0, s]
        goal = jnp.where(slot == s, label, goal)
    number = jnp.where(goal >= 0, (goal & 15) + 1, 0)
    goal = jnp.where(goal >= 0, (goal >> 4) * 16 + (lane & 15), -1)[0:1]
    rest_scr[...] = jnp.zeros(rest_scr.shape, BF)
    for k in range(4):
        rest_scr[16 * k : 16 * k + 16, :] = x_ref[k, MAIN : MAIN + 16, :]
    rest_scr[64:80, :] = jnp.where(iota((16, positions), 0) == 0, number, 0).astype(F32).astype(BF)
    step = 256
    for r in range(0, out_ref.shape[0] * PIECE, step):
        pick = jnp.where(iota((step, positions), 0) + r == goal, 1.0, 0.0).astype(BF)
        first = slice(r // PIECE, (r + step) // PIECE)
        for k in range(4):
            left = k * MAIN
            moved = dot_last(pick, x_ref[k, 0:MAIN, :]).astype(BF)
            out_ref[first, :, left : left + MAIN] = moved.reshape(step // PIECE, PIECE, MAIN)
        moved = dot_last(pick, rest_scr[...]).astype(BF)
        out_ref[first, :, 4 * MAIN :] = moved.reshape(step // PIECE, PIECE, 128)


def pack(labels, columns, peers):
    return pl.pallas_call(
        pack_kernel,
        out_shape=jax.ShapeDtypeStruct((peers, PIECE, 4 * MAIN + 128), BF),
        in_specs=[
            pl.BlockSpec(memory_space=pltpu.SMEM),
            pl.BlockSpec(memory_space=pltpu.VMEM),
        ],
        out_specs=pl.BlockSpec(memory_space=pltpu.VMEM),
        scratch_shapes=[pltpu.VMEM((128, columns.shape[2]), BF)],
        compiler_params=params(),
        name="pack_pieces",
    )(labels, columns)


def receive_kernel(source_ref, in_ref, weight_ref, rows_ref, part_ref, rest_scr, left_scr, stack_scr, weight_scr):
    @pl.when(pl.program_id(0) == 0)
    def _():
        for i in range(NPIECE):
            rest_scr[16 * i : 16 * i + 16, :] = in_ref[source_ref[i], :, 4 * MAIN :]
        rest = rest_scr[...]
        column = iota((MAIN, 8 * GPAD), 1)
        inside = (column & 63) < GROUP
        feature = (column >> 6) * GROUP + (column & 63)
        spread = jnp.where((feature == iota((MAIN, 8 * GPAD), 0)) & inside, 1.0, 0.0).astype(BF)
        row = iota((256, 256), 0)
        wanted = (row & 1) * 128 + (row >> 5) * 16 + ((row >> 1) & 15)
        order = jnp.where(iota((256, 256), 1) == wanted, 1.0, 0.0).astype(BF)
        lane = iota((128, 8 * GPAD), 0)
        for e in range(2):
            for u in range(2):
                k = 2 * e + u
                for i in range(NPIECE):
                    left_scr[16 * i : 16 * i + 16, :] = in_ref[source_ref[i], :, k * MAIN : (k + 1) * MAIN]
                spread_rest = jnp.where(
                    (feature[0:128] == lane + (MAIN - 16 * k)) & inside[0:128] & (lane >= 16 * k) & (lane < 16 * k + 16),
                    1.0,
                    0.0,
                ).astype(BF)
                wide = (dot(left_scr[...], spread) + dot(rest, spread_rest)).astype(BF)
                stack_scr[0, u * 128 : (u + 1) * 128, :] = wide[0:128]
                stack_scr[1, u * 128 : (u + 1) * 128, :] = wide[128:256]
            for half in range(2):
                lower = e * 512 + half * 256
                rows_ref[lower : lower + 256, :] = dot(order, stack_scr[half]).astype(BF)
        weight_scr[...] = jnp.zeros(weight_scr.shape, BF)

    for c in range(2):
        for x in range(4):
            lower = (2 * x + c) * GPAD
            weight_scr[lower : lower + GROUP, :] = weight_ref[c, x, 0]
    part_ref[0] = dot(rows_ref[...], weight_scr[...]).astype(BF)


def receive(source, arrived, weight):
    return pl.pallas_call(
        receive_kernel,
        grid=(8,),
        out_shape=(
            jax.ShapeDtypeStruct((1024, 512), BF),
            jax.ShapeDtypeStruct((8, 1024, 256), BF),
        ),
        in_specs=[
            pl.BlockSpec(memory_space=pltpu.SMEM),
            pl.BlockSpec(memory_space=pltpu.VMEM),
            pl.BlockSpec((2, 4, 1, GROUP, 256), lambda a: (0, 0, a, 0, 0)),
        ],
        out_specs=(
            pl.BlockSpec((1024, 512), lambda a: (0, 0)),
            pl.BlockSpec((1, 1024, 256), lambda a: (a, 0, 0)),
        ),
        scratch_shapes=[
            pltpu.VMEM((256, 128), BF),
            pltpu.VMEM((256, MAIN), BF),
            pltpu.VMEM((2, 256, 512), BF),
            pltpu.VMEM((8 * GPAD, 256), BF),
        ],
        compiler_params=params(),
        name="receive_pieces",
    )(source, arrived, weight)


def forward_kernel(x_ref, p_ref, att_ref, a_ref, q_scr, vt_scr, a_scr):
    tail_row = iota((16, 128), 0) == 0
    q_scr[0:1024, :] = x_ref[0, 0, 0:1024, :]
    q_scr[1024:QPAD, :] = jnp.zeros((128, 128), BF)
    q_scr[1024:1040, :] = jnp.where(tail_row, x_ref[0, 0, 1024:1025, :].astype(F32), 0.0).astype(BF)
    key = x_ref[0, 1, 0:1024, :]
    key_tail = jnp.where(tail_row, x_ref[0, 1, 1024:1025, :].astype(F32), 0.0).astype(BF)
    vt_scr[...] = x_ref[0, 2, 0:1024, :].astype(F32).T.astype(BF)
    value_tail = jnp.where(tail_row, x_ref[0, 2, 1024:1025, :].astype(F32), 0.0).astype(BF)
    first = iota((16, QBLK), 0) == 0
    for j in range(QPAD // QBLK):
        span = slice(j * QBLK, (j + 1) * QBLK)
        query = q_scr[span, :]
        score = dot_last(key, query) * SCALE
        score_tail = (dot_last(key_tail, query) * SCALE)[0:1]
        top = jnp.maximum(jnp.max(score, axis=0, keepdims=True), score_tail)
        shifted = jnp.exp(score - top)
        shifted_tail = jnp.exp(score_tail - top)
        inverse = 1.0 / (jnp.sum(shifted, axis=0, keepdims=True) + shifted_tail)
        low = (shifted * inverse).astype(BF)
        low_tail = jnp.where(first, shifted_tail * inverse, 0.0).astype(BF)
        p_ref[0, 0:1024, span] = low
        p_ref[0, 1024:KPAD, span] = low_tail
        att = (dot(vt_scr[...], low) + dot_first(value_tail, low_tail)).T.astype(BF)
        att_ref[span, :] = att
        a_scr[span, :] = att.astype(F32)
    moved = a_scr[pl.ds(1, 1024), :].astype(BF)
    for i in range(NPIECE):
        for e in range(2):
            a_ref[512 * e + 32 * i : 512 * e + 32 * i + 32, :] = moved[64 * i + 32 * e : 64 * i + 32 * e + 32]


def forward(head_inputs):
    return pl.pallas_call(
        forward_kernel,
        grid=(2,),
        out_shape=(
            jax.ShapeDtypeStruct((2, KPAD, QPAD), BF),
            jax.ShapeDtypeStruct((QPAD, 256), BF),
            jax.ShapeDtypeStruct((PATCHES, 256), BF),
        ),
        in_specs=[pl.BlockSpec((1, 3, TT, HD), lambda h: (0, 0, 0, h))],
        out_specs=(
            pl.BlockSpec((1, KPAD, QPAD), lambda h: (h, 0, 0)),
            pl.BlockSpec((QPAD, HD), lambda h: (0, h)),
            pl.BlockSpec((PATCHES, HD), lambda h: (0, h)),
        ),
        scratch_shapes=[
            pltpu.VMEM((QPAD, HD), BF),
            pltpu.VMEM((HD, 1024), BF),
            pltpu.VMEM((QPAD, HD), F32),
        ],
        compiler_params=params(),
        cost_estimate=pl.CostEstimate(flops=12 * 10**9, bytes_accessed=8 * 10**6, transcendentals=2 * 10**6),
        name="attend",
    )(head_inputs)


def backward_kernel(x_ref, p_ref, att_ref, o_ref, out_ref, q_scr, kt_scr, g_scr, dq_scr, dk_scr, dv_scr, dkt_scr, dvt_scr):
    tail_row = iota((16, 128), 0) == 0
    q_scr[0:1024, :] = x_ref[0, 0, 0:1024, :]
    q_scr[1024:QPAD, :] = jnp.zeros((128, 128), BF)
    q_scr[1024:1040, :] = jnp.where(tail_row, x_ref[0, 0, 1024:1025, :].astype(F32), 0.0).astype(BF)
    kt_scr[...] = x_ref[0, 1, 0:1024, :].astype(F32).T.astype(BF)
    key_tail = jnp.where(tail_row, x_ref[0, 1, 1024:1025, :].astype(F32), 0.0).astype(BF)
    value = x_ref[0, 2, 0:1024, :]
    value_tail = jnp.where(tail_row, x_ref[0, 2, 1024:1025, :].astype(F32), 0.0).astype(BF)
    g_scr[0:8, :] = jnp.zeros((8, HD), F32)
    g_scr[1024 : QPAD, :] = jnp.zeros((QPAD - 1024, HD), F32)
    for i in range(NPIECE):
        g_scr[pl.ds(1 + 64 * i, 32), :] = o_ref[32 * i : 32 * i + 32, :].astype(F32)
        g_scr[pl.ds(33 + 64 * i, 32), :] = o_ref[512 + 32 * i : 544 + 32 * i, :].astype(F32)
    for j in range(QPAD // QBLK):
        span = slice(j * QBLK, (j + 1) * QBLK)
        query = q_scr[span, :]
        grad_wide = g_scr[span, :]
        grad = grad_wide.astype(BF)
        delta = jnp.sum((grad_wide * att_ref[span, :].astype(F32)).T, axis=0, keepdims=True)
        low = p_ref[0, 0:1024, span]
        low_tail = p_ref[0, 1024:KPAD, span]
        inner = (low.astype(F32) * (dot_last(value, grad) - delta)).astype(BF)
        inner_tail = (low_tail.astype(F32) * (dot_last(value_tail, grad) - delta)).astype(BF)
        dq = (dot(kt_scr[...], inner) + dot_first(key_tail, inner_tail)) * SCALE
        dq_scr[span, :] = dq.T.astype(BF)
        dk, dkt = dot(inner, query), dot(inner_tail, query)
        dv, dvt = dot(low, grad), dot(low_tail, grad)
        if j == 0:
            dk_scr[...], dkt_scr[...], dv_scr[...], dvt_scr[...] = dk, dkt, dv, dvt
        else:
            dk_scr[...] += dk
            dkt_scr[...] += dkt
            dv_scr[...] += dv
            dvt_scr[...] += dvt
    out_ref[0, 0, 0:1024, :] = dq_scr[0:1024, :]
    out_ref[0, 0, 1024:1025, :] = dq_scr[1024:1040, :][0:1]
    out_ref[0, 1, 0:1024, :] = (dk_scr[...] * SCALE).astype(BF)
    out_ref[0, 1, 1024:1025, :] = (dkt_scr[...] * SCALE).astype(BF)[0:1]
    out_ref[0, 2, 0:1024, :] = dv_scr[...].astype(BF)
    out_ref[0, 2, 1024:1025, :] = dvt_scr[...].astype(BF)[0:1]


def backward(head_inputs, probs, att, out_grad):
    return pl.pallas_call(
        backward_kernel,
        grid=(2,),
        out_shape=jax.ShapeDtypeStruct((1, 3, TT, 256), BF),
        in_specs=[
            pl.BlockSpec((1, 3, TT, HD), lambda h: (0, 0, 0, h)),
            pl.BlockSpec((1, KPAD, QPAD), lambda h: (h, 0, 0)),
            pl.BlockSpec((QPAD, HD), lambda h: (0, h)),
            pl.BlockSpec((PATCHES, HD), lambda h: (0, h)),
        ],
        out_specs=pl.BlockSpec((1, 3, TT, HD), lambda h: (0, 0, 0, h)),
        scratch_shapes=[
            pltpu.VMEM((QPAD, HD), BF),
            pltpu.VMEM((HD, 1024), BF),
            pltpu.VMEM((QPAD, HD), F32),
            pltpu.VMEM((QPAD, HD), BF),
            pltpu.VMEM((1024, HD), F32),
            pltpu.VMEM((1024, HD), F32),
            pltpu.VMEM((16, HD), F32),
            pltpu.VMEM((16, HD), F32),
        ],
        compiler_params=params(),
        name="attend_backward",
    )(head_inputs, probs, att, out_grad)


def weight_kernel(core_ref, r_ref, a_ref, keep_ref, send_ref, t_scr, sum_scr):
    @pl.when(pl.program_id(0) == 0)
    def _():
        t_scr[...] = r_ref[...].astype(F32).T.astype(BF)

    sum_scr[...] = dot(t_scr[...], a_ref[0])
    core = core_ref[0]
    for x in range(4):
        mine = pl.multiple_of((2 * x + core) * GPAD, GPAD)
        other = pl.multiple_of((2 * x + 1 - core) * GPAD, GPAD)
        keep_ref[0, x] = sum_scr[pl.ds(mine, GPAD), :][0:GROUP]
        send_ref[0, x] = sum_scr[pl.ds(other, GPAD), :][0:GROUP].astype(BF)


def weight_parts(core, rows, gathered):
    return pl.pallas_call(
        weight_kernel,
        grid=(8,),
        out_shape=(
            jax.ShapeDtypeStruct((8, 4, GROUP, 256), F32),
            jax.ShapeDtypeStruct((8, 4, GROUP, 256), BF),
        ),
        in_specs=[
            pl.BlockSpec(memory_space=pltpu.SMEM),
            pl.BlockSpec((1024, 512), lambda a: (0, 0)),
            pl.BlockSpec((1, PATCHES, 256), lambda a: (a, 0, 0)),
        ],
        out_specs=(
            pl.BlockSpec((1, 4, GROUP, 256), lambda a: (a, 0, 0, 0)),
            pl.BlockSpec((1, 4, GROUP, 256), lambda a: (a, 0, 0, 0)),
        ),
        scratch_shapes=[
            pltpu.VMEM((512, 1024), BF),
            pltpu.VMEM((512, 256), F32),
        ],
        compiler_params=params(),
        name="weight_parts",
    )(core, rows, gathered)


def per_device(head_inputs, out_weight, sequence_gradient, slot_labels):
    peers = 64
    swap = [(z * 8 + y, y * 8 + z) for z in range(8) for y in range(8)]
    weight = lax.ppermute(out_weight, ("z", "y"), swap)
    outgoing = pack(slot_labels, sequence_gradient.transpose(0, 2, 1), peers)
    outgoing, weight = lax.optimization_barrier((outgoing, weight))
    weight = lax.all_to_all(jnp.broadcast_to(weight[None], (8, GROUP, 256)), "z", 0, 0, tiled=True)
    probs, att, parts = forward(head_inputs)
    outgoing, weight, parts = lax.optimization_barrier((outgoing, weight, parts))

    arrived = lax.all_to_all(outgoing, SHARDS, 0, 0, tiled=True)
    weight = lax.all_gather(weight, ("c", "x"), axis=0)
    weight = weight.reshape(2, 4, 8, GROUP, 256)
    gathered = lax.all_gather(parts, "y", axis=0)

    ids = arrived[:, 0, 4 * MAIN + 64].astype(jnp.int32) - 1
    wanted = jnp.arange(NPIECE, dtype=jnp.int32)
    source = jnp.sum(
        jnp.where(ids[None, :] == wanted[:, None], jnp.arange(peers, dtype=jnp.int32)[None, :], 0), axis=1
    )
    rows, part = receive(source, arrived, weight)
    out_grad = lax.psum_scatter(part, "y", scatter_dimension=0, tiled=True)[0]

    core = lax.axis_index("c").astype(jnp.int32)[None]
    keep, send = weight_parts(core, rows, gathered)
    got = lax.ppermute(send, "c", [(0, 1), (1, 0)])
    both = (keep + got.astype(F32)).astype(BF).reshape(32, GROUP, 256)
    spread = lax.all_to_all(both, ("z", "x"), 0, 0, tiled=True)
    summed = jnp.sum(spread.astype(F32), axis=0) * (1.0 / math.sqrt(65536))
    weight_gradient = lax.ppermute(summed, ("z", "y"), swap)

    head_gradient = backward(head_inputs, probs, att, out_grad)
    return head_gradient, weight_gradient


def solution(mesh):
    fine = Mesh(mesh.devices.reshape(8, 4, 2, 8), ("z", "x", "c", "y"))
    return jax.shard_map(
        per_device,
        mesh=fine,
        in_specs=(
            P(SHARDS, None, None, "y"),
            P(SHARDS, "y"),
            P(None, SHARDS, "y"),
            P(SHARDS, None),
        ),
        out_specs=(P(SHARDS, None, None, "y"), P(SHARDS, "y")),
        check_vma=False,
    )
```

```python
import functools
import math

import jax
import jax.numpy as jnp
from jax import lax
from jax.experimental import pallas as pl
from jax.experimental.pallas import tpu as pltpu
from jax.sharding import Mesh, PartitionSpec as P

HD = 128
TT = 1025
PATCHES = 1024
KPAD = 1040
QPAD = 1152
QBLK = 384
PIECE = 16
NPIECE = 16
MAIN = 384
GROUP = 50
GPAD = 64
GSEND = 56
BF = jnp.bfloat16
F32 = jnp.float32
SHARDS = ("z", "x", "c")
SCALE = HD ** (-0.5)


def dot(left, right):
    return jnp.dot(left, right, preferred_element_type=F32)


def dot_last(left, right):
    return lax.dot_general(left, right, (((1,), (1,)), ((), ())), preferred_element_type=F32)


def dot_first(left, right):
    return lax.dot_general(left, right, (((0,), (0,)), ((), ())), preferred_element_type=F32)


def iota(shape, axis):
    return lax.broadcasted_iota(jnp.int32, shape, axis)


def params(mebibytes):
    return pltpu.CompilerParams(vmem_limit_bytes=mebibytes * 1024 * 1024)


def pack_kernel(label_ref, x_ref, out_ref, rest_scr, goal_scr):
    positions = x_ref.shape[2]

    @pl.when(pl.program_id(0) == 0)
    def _():
        lane = iota((16, positions), 1)
        slot = lane >> 4
        goal = jnp.full((16, positions), -1, jnp.int32)
        for s in range(label_ref.shape[1]):
            goal = jnp.where(slot == s, label_ref[0, s], goal)
        number = jnp.where(goal >= 0, (goal & 15) + 1, 0)
        goal_scr[...] = jnp.where(goal >= 0, (goal >> 4) * 16 + (lane & 15), -1)
        rest_scr[...] = jnp.zeros(rest_scr.shape, BF)
        for k in range(4):
            rest_scr[16 * k : 16 * k + 16, :] = x_ref[k, MAIN : MAIN + 16, :]
        rest_scr[64:80, :] = jnp.where(iota((16, positions), 0) == 0, number, 0).astype(F32).astype(BF)

    step = out_ref.shape[0] * PIECE
    row = iota((step, positions), 0) + pl.program_id(0) * step
    pick = jnp.where(row == goal_scr[0:1, :], 1.0, 0.0).astype(BF)
    for k in range(4):
        moved = dot_last(pick, x_ref[k, 0:MAIN, :]).astype(BF)
        out_ref[:, :, k * MAIN : (k + 1) * MAIN] = moved.reshape(step // PIECE, PIECE, MAIN)
    moved = dot_last(pick, rest_scr[...]).astype(BF)
    out_ref[:, :, 4 * MAIN :] = moved.reshape(step // PIECE, PIECE, 128)


def pack(labels, columns, peers):
    features, positions = columns.shape[1:]
    return pl.pallas_call(
        pack_kernel,
        grid=(4,),
        out_shape=jax.ShapeDtypeStruct((peers, PIECE, 4 * MAIN + 128), BF),
        in_specs=[
            pl.BlockSpec(memory_space=pltpu.SMEM),
            pl.BlockSpec((4, features, positions), lambda r: (0, 0, 0)),
        ],
        out_specs=pl.BlockSpec((peers // 4, PIECE, 4 * MAIN + 128), lambda r: (r, 0, 0)),
        scratch_shapes=[pltpu.VMEM((128, positions), BF), pltpu.VMEM((16, positions), jnp.int32)],
        compiler_params=params(60),
        name="pack_pieces",
    )(labels, columns)


def assemble_kernel(in_ref, out_ref):
    out_ref[...] = jnp.zeros(out_ref.shape, BF)
    for a in range(8):
        for g in range(8):
            out_ref[a, g * GPAD : g * GPAD + GROUP, :] = in_ref[8 * a + g]


def assemble(arrived):
    vmem = pl.BlockSpec(memory_space=pltpu.VMEM)
    return pl.pallas_call(
        assemble_kernel,
        out_shape=jax.ShapeDtypeStruct((8, 8 * GPAD, 256), BF),
        in_specs=[vmem],
        out_specs=vmem,
        compiler_params=params(24),
        cost_estimate=pl.CostEstimate(flops=48 * 10**9, bytes_accessed=4 * 10**6, transcendentals=0),
        name="assemble_weight",
    )(arrived)


def receive_kernel(in_ref, weight_ref, rows_ref, part_ref, placed_scr, stack_scr):
    @pl.when(pl.program_id(0) == 0)
    def _():
        slots = in_ref.shape[0]
        numbers = in_ref[:, 4 * MAIN :].astype(F32).T[64:65]
        row = iota((256, slots), 0)
        wanted = (numbers == ((row >> 4) + 1).astype(F32)) & ((iota((256, slots), 1) & 15) == (row & 15))
        pick = jnp.where(wanted, 1.0, 0.0).astype(BF)
        for left in range(0, 4 * MAIN, MAIN):
            placed_scr[:, left : left + MAIN] = dot(pick, in_ref[:, left : left + MAIN]).astype(BF)
        rest = dot(pick, in_ref[:, 4 * MAIN :]).astype(BF)
        column = iota((MAIN, 8 * GPAD), 1)
        inside = (column & 63) < GROUP
        feature = (column >> 6) * GROUP + (column & 63)
        spread = jnp.where((feature == iota((MAIN, 8 * GPAD), 0)) & inside, 1.0, 0.0).astype(BF)
        row = iota((256, 256), 0)
        source = (row & 1) * 128 + (row >> 5) * 16 + ((row >> 1) & 15)
        order = jnp.where(iota((256, 256), 1) == source, 1.0, 0.0).astype(BF)
        lane = iota((128, 8 * GPAD), 0)
        for e in range(2):
            for u in range(2):
                k = 2 * e + u
                spread_rest = jnp.where(
                    (feature[0:128] == lane + (MAIN - 16 * k)) & inside[0:128] & (lane >= 16 * k) & (lane < 16 * k + 16),
                    1.0,
                    0.0,
                ).astype(BF)
                wide = (dot(placed_scr[:, k * MAIN : (k + 1) * MAIN], spread) + dot(rest, spread_rest)).astype(BF)
                stack_scr[0, u * 128 : (u + 1) * 128, :] = wide[0:128]
                stack_scr[1, u * 128 : (u + 1) * 128, :] = wide[128:256]
            for half in range(2):
                lower = e * 512 + half * 256
                rows_ref[lower : lower + 256, :] = dot(order, stack_scr[half]).astype(BF)

    for a in range(2):
        part_ref[a] = dot(rows_ref[...], weight_ref[a]).astype(BF)


def receive(arrived, weight):
    slots = arrived.shape[0]
    return pl.pallas_call(
        receive_kernel,
        grid=(4,),
        out_shape=(
            jax.ShapeDtypeStruct((1024, 512), BF),
            jax.ShapeDtypeStruct((8, 1024, 256), BF),
        ),
        in_specs=[
            pl.BlockSpec(memory_space=pltpu.VMEM),
            pl.BlockSpec((2, 8 * GPAD, 256), lambda a: (a, 0, 0)),
        ],
        out_specs=(
            pl.BlockSpec((1024, 512), lambda a: (0, 0)),
            pl.BlockSpec((2, 1024, 256), lambda a: (a, 0, 0)),
        ),
        scratch_shapes=[
            pltpu.VMEM((256, 4 * MAIN), BF),
            pltpu.VMEM((2, 256, 512), BF),
        ],
        compiler_params=params(60),
        name="receive_pieces",
    )(arrived, weight)


def forward_kernel(x_ref, p_ref, att_ref, a_ref, q_scr, vt_scr, a_scr):
    tail_row = iota((16, 128), 0) == 0
    q_scr[0:1024, :] = x_ref[0, 0, 0:1024, :]
    q_scr[1024:QPAD, :] = jnp.zeros((128, 128), BF)
    q_scr[1024:1040, :] = jnp.where(tail_row, x_ref[0, 0, 1024:1025, :].astype(F32), 0.0).astype(BF)
    key = x_ref[0, 1, 0:1024, :]
    key_tail = jnp.where(tail_row, x_ref[0, 1, 1024:1025, :].astype(F32), 0.0).astype(BF)
    vt_scr[...] = x_ref[0, 2, 0:1024, :].astype(F32).T.astype(BF)
    value_tail = jnp.where(tail_row, x_ref[0, 2, 1024:1025, :].astype(F32), 0.0).astype(BF)
    first = iota((16, QBLK), 0) == 0
    for j in range(QPAD // QBLK):
        span = slice(j * QBLK, (j + 1) * QBLK)
        query = q_scr[span, :]
        score = dot_last(key, query) * SCALE
        score_tail = (dot_last(key_tail, query) * SCALE)[0:1]
        top = jnp.maximum(jnp.max(score, axis=0, keepdims=True), score_tail)
        shifted = jnp.exp(score - top)
        shifted_tail = jnp.exp(score_tail - top)
        inverse = 1.0 / (jnp.sum(shifted, axis=0, keepdims=True) + shifted_tail)
        low = (shifted * inverse).astype(BF)
        low_tail = jnp.where(first, shifted_tail * inverse, 0.0).astype(BF)
        p_ref[0, 0:1024, span] = low
        p_ref[0, 1024:KPAD, span] = low_tail
        att = (dot(vt_scr[...], low) + dot_first(value_tail, low_tail)).T.astype(BF)
        att_ref[span, :] = att
        a_scr[span, :] = att.astype(F32)
    moved = a_scr[pl.ds(1, 1024), :].astype(BF)
    for i in range(NPIECE):
        for e in range(2):
            a_ref[512 * e + 32 * i : 512 * e + 32 * i + 32, :] = moved[64 * i + 32 * e : 64 * i + 32 * e + 32]


def forward(head_inputs):
    return pl.pallas_call(
        forward_kernel,
        grid=(2,),
        out_shape=(
            jax.ShapeDtypeStruct((2, KPAD, QPAD), BF),
            jax.ShapeDtypeStruct((QPAD, 256), BF),
            jax.ShapeDtypeStruct((PATCHES, 256), BF),
        ),
        in_specs=[pl.BlockSpec((1, 3, TT, HD), lambda h: (0, 0, 0, h))],
        out_specs=(
            pl.BlockSpec((1, KPAD, QPAD), lambda h: (h, 0, 0)),
            pl.BlockSpec((QPAD, HD), lambda h: (0, h)),
            pl.BlockSpec((PATCHES, HD), lambda h: (0, h)),
        ),
        scratch_shapes=[
            pltpu.VMEM((QPAD, HD), BF),
            pltpu.VMEM((HD, 1024), BF),
            pltpu.VMEM((QPAD, HD), F32),
        ],
        compiler_params=params(50),
        cost_estimate=pl.CostEstimate(flops=2 * 10**9, bytes_accessed=8 * 10**6, transcendentals=2 * 10**6),
        name="attend",
    )(head_inputs)


def backward_kernel(x_ref, p_ref, att_ref, o_ref, out_ref, q_scr, kt_scr, g_scr):
    tail_row = iota((16, 128), 0) == 0
    q_scr[0:1024, :] = x_ref[0, 0, 0:1024, :]
    q_scr[1024:QPAD, :] = jnp.zeros((128, 128), BF)
    q_scr[1024:1040, :] = jnp.where(tail_row, x_ref[0, 0, 1024:1025, :].astype(F32), 0.0).astype(BF)
    kt_scr[...] = x_ref[0, 1, 0:1024, :].astype(F32).T.astype(BF)
    key_tail = jnp.where(tail_row, x_ref[0, 1, 1024:1025, :].astype(F32), 0.0).astype(BF)
    value = x_ref[0, 2, 0:1024, :]
    value_tail = jnp.where(tail_row, x_ref[0, 2, 1024:1025, :].astype(F32), 0.0).astype(BF)
    g_scr[0:8, :] = jnp.zeros((8, HD), F32)
    g_scr[1024 : QPAD, :] = jnp.zeros((QPAD - 1024, HD), F32)
    for i in range(NPIECE):
        g_scr[pl.ds(1 + 64 * i, 32), :] = o_ref[32 * i : 32 * i + 32, :].astype(F32)
        g_scr[pl.ds(33 + 64 * i, 32), :] = o_ref[512 + 32 * i : 544 + 32 * i, :].astype(F32)
    query = q_scr[...]
    grad_wide = g_scr[...]
    grad = grad_wide.astype(BF)
    delta = jnp.sum((grad_wide * att_ref[...].astype(F32)).T, axis=0, keepdims=True)
    low_tail = p_ref[0, 1024:KPAD, :]
    inner_tail = (low_tail.astype(F32) * (dot_last(value_tail, grad) - delta)).astype(BF)
    dq = dot_first(key_tail, inner_tail)
    out_ref[0, 1, 1024:1025, :] = (dot(inner_tail, query) * SCALE).astype(BF)[0:1]
    out_ref[0, 2, 1024:1025, :] = dot(low_tail, grad).astype(BF)[0:1]
    low = p_ref[0, 0:1024, :]
    out_ref[0, 2, 0:1024, :] = dot(low, grad).astype(BF)
    inner = (low.astype(F32) * (dot_last(value, grad) - delta)).astype(BF)
    out_ref[0, 1, 0:1024, :] = (dot(inner, query) * SCALE).astype(BF)
    dq = dq + dot(kt_scr[...], inner)
    dq = (dq * SCALE).T.astype(BF)
    out_ref[0, 0, 0:1024, :] = dq[0:1024]
    out_ref[0, 0, 1024:1025, :] = dq[1024:1040][0:1]


def backward(head_inputs, probs, att, out_grad):
    return pl.pallas_call(
        backward_kernel,
        grid=(2,),
        out_shape=jax.ShapeDtypeStruct((1, 3, TT, 256), BF),
        in_specs=[
            pl.BlockSpec((1, 3, TT, HD), lambda h: (0, 0, 0, h)),
            pl.BlockSpec((1, KPAD, QPAD), lambda h: (h, 0, 0)),
            pl.BlockSpec((QPAD, HD), lambda h: (0, h)),
            pl.BlockSpec((PATCHES, HD), lambda h: (0, h)),
        ],
        out_specs=pl.BlockSpec((1, 3, TT, HD), lambda h: (0, 0, 0, h)),
        scratch_shapes=[
            pltpu.VMEM((QPAD, HD), BF),
            pltpu.VMEM((HD, 1024), BF),
            pltpu.VMEM((QPAD, HD), F32),
        ],
        compiler_params=params(60),
        name="attend_backward",
    )(head_inputs, probs, att, out_grad)


def weight_kernel(place_ref, r_ref, *refs):
    parts = refs[:8]
    keep_ref, send_ref, t_scr, sum_scr, part_scr, sems = refs[8:]
    copies = [pltpu.make_async_copy(parts[n], part_scr.at[n], sems.at[n]) for n in range(8)]
    for copy in copies:
        copy.start()
    t_scr[...] = r_ref[...].astype(F32).T.astype(BF)
    core = place_ref[0]
    for n in range(8):
        block = (place_ref[1] - n) & 7
        copies[n].wait()
        sum_scr[...] = dot(t_scr[...], part_scr[n])
        for x in range(4):
            mine = pl.multiple_of((2 * x + core) * GPAD, GPAD)
            other = pl.multiple_of((2 * x + 1 - core) * GPAD, GPAD)
            keep_ref[4 * block + x] = sum_scr[pl.ds(mine, GSEND), :]
            send_ref[4 * block + x] = sum_scr[pl.ds(other, GSEND), :].astype(BF)


def weight_parts(place, rows, gathered):
    vmem = pl.BlockSpec(memory_space=pltpu.VMEM)
    return pl.pallas_call(
        weight_kernel,
        out_shape=(
            jax.ShapeDtypeStruct((32, GSEND, 256), F32),
            jax.ShapeDtypeStruct((32, GSEND, 256), BF),
        ),
        in_specs=[pl.BlockSpec(memory_space=pltpu.SMEM), vmem] + [pl.BlockSpec(memory_space=pl.ANY)] * 8,
        out_specs=(vmem, vmem),
        scratch_shapes=[
            pltpu.VMEM((512, 1024), BF),
            pltpu.VMEM((512, 256), F32),
            pltpu.VMEM((8, PATCHES, 256), BF),
            pltpu.SemaphoreType.DMA((8,)),
        ],
        compiler_params=params(60),
        name="weight_parts",
    )(place, rows, *gathered)


def ring(count, step):
    return [(i, (i + step) % count) for i in range(count)]


def per_device(head_inputs, out_weight, sequence_gradient, slot_labels):
    peers = 64
    swap = [(z * 8 + y, y * 8 + z) for z in range(8) for y in range(8)]
    weight = lax.ppermute(out_weight, ("z", "y"), swap)
    place = jnp.stack([lax.axis_index(name).astype(jnp.int32) for name in ("c", "y")])
    outgoing = pack(slot_labels, sequence_gradient.transpose(0, 2, 1), peers)
    outgoing, head_inputs, weight = lax.optimization_barrier((outgoing, head_inputs, weight))
    weight = assemble(lax.all_gather(weight, SHARDS, axis=0))
    arrived = lax.all_to_all(outgoing, SHARDS, 0, 0, tiled=True)

    probs, att, parts = forward(head_inputs)
    back = [parts]
    for _ in range(4):
        back.append(lax.ppermute(back[-1], "y", ring(8, 1)))
    ahead = [parts]
    for _ in range(3):
        ahead.append(lax.ppermute(ahead[-1], "y", ring(8, -1)))
    arrived, *gathered = lax.optimization_barrier((arrived, *back, *ahead[:0:-1]))

    rows, part = receive(arrived.reshape(peers * PIECE, 4 * MAIN + 128), weight)
    out_grad = lax.psum_scatter(part, "y", scatter_dimension=0, tiled=True)[0]

    keep, send = weight_parts(place, rows, gathered)
    got = lax.ppermute(send, "c", [(0, 1), (1, 0)])
    both = (keep + got.astype(F32)).astype(BF)
    spread = lax.all_to_all(both, ("z", "x"), 0, 0, tiled=True)
    summed = jnp.sum(spread.astype(F32), axis=0)[:GROUP] * (1.0 / math.sqrt(65536))
    weight_gradient = lax.ppermute(summed, ("z", "y"), swap)

    head_gradient = backward(head_inputs, probs, att, out_grad)
    return head_gradient, weight_gradient


def solution(mesh):
    fine = Mesh(mesh.devices.reshape(8, 4, 2, 8), ("z", "x", "c", "y"))
    return jax.shard_map(
        per_device,
        mesh=fine,
        in_specs=(
            P(SHARDS, None, None, "y"),
            P(SHARDS, "y"),
            P(None, SHARDS, "y"),
            P(SHARDS, None),
        ),
        out_specs=(P(SHARDS, None, None, "y"), P(SHARDS, "y")),
        check_vma=False,
    )
```

```python
import functools
import math

import jax
import jax.numpy as jnp
from jax import lax
from jax.experimental import pallas as pl
from jax.experimental.pallas import tpu as pltpu
from jax.sharding import Mesh, PartitionSpec as P

HD = 128
TT = 1025
PATCHES = 1024
KPAD = 1040
QPAD = 1152
QBLK = 384
PIECE = 16
NPIECE = 16
MAIN = 384
GROUP = 50
GPAD = 64
GSEND = 56
BF = jnp.bfloat16
F32 = jnp.float32
SHARDS = ("z", "x", "c")
SCALE = HD ** (-0.5)


def dot(left, right):
    return jnp.dot(left, right, preferred_element_type=F32)


def dot_last(left, right):
    return lax.dot_general(left, right, (((1,), (1,)), ((), ())), preferred_element_type=F32)


def dot_first(left, right):
    return lax.dot_general(left, right, (((0,), (0,)), ((), ())), preferred_element_type=F32)


def iota(shape, axis):
    return lax.broadcasted_iota(jnp.int32, shape, axis)


def params(mebibytes):
    return pltpu.CompilerParams(vmem_limit_bytes=mebibytes * 1024 * 1024)


def pack_kernel(label_ref, x_ref, out_ref, rest_scr, goal_scr):
    positions = x_ref.shape[2]

    @pl.when(pl.program_id(0) == 0)
    def _():
        lane = iota((16, positions), 1)
        slot = lane >> 4
        goal = jnp.full((16, positions), -1, jnp.int32)
        for s in range(label_ref.shape[1]):
            goal = jnp.where(slot == s, label_ref[0, s], goal)
        number = jnp.where(goal >= 0, (goal & 15) + 1, 0)
        goal_scr[...] = jnp.where(goal >= 0, (goal >> 4) * 16 + (lane & 15), -1)
        rest_scr[...] = jnp.zeros(rest_scr.shape, BF)
        for k in range(4):
            rest_scr[16 * k : 16 * k + 16, :] = x_ref[k, MAIN : MAIN + 16, :]
        rest_scr[64:80, :] = jnp.where(iota((16, positions), 0) == 0, number, 0).astype(F32).astype(BF)

    step = out_ref.shape[0] * PIECE
    row = iota((step, positions), 0) + pl.program_id(0) * step
    pick = jnp.where(row == goal_scr[0:1, :], 1.0, 0.0).astype(BF)
    for k in range(0, 4, 2):
        moved = dot_last(pick, x_ref[k : k + 2, 0:MAIN, :].reshape(2 * MAIN, positions)).astype(BF)
        out_ref[:, :, k * MAIN : (k + 2) * MAIN] = moved.reshape(step // PIECE, PIECE, 2 * MAIN)
    moved = dot_last(pick, rest_scr[...]).astype(BF)
    out_ref[:, :, 4 * MAIN :] = moved.reshape(step // PIECE, PIECE, 128)


def pack(labels, columns, peers):
    features, positions = columns.shape[1:]
    return pl.pallas_call(
        pack_kernel,
        grid=(2,),
        out_shape=jax.ShapeDtypeStruct((peers, PIECE, 4 * MAIN + 128), BF),
        in_specs=[
            pl.BlockSpec(memory_space=pltpu.SMEM),
            pl.BlockSpec((4, features, positions), lambda r: (0, 0, 0)),
        ],
        out_specs=pl.BlockSpec((peers // 2, PIECE, 4 * MAIN + 128), lambda r: (r, 0, 0)),
        scratch_shapes=[pltpu.VMEM((128, positions), BF), pltpu.VMEM((16, positions), jnp.int32)],
        compiler_params=params(60),
        name="pack_pieces",
    )(labels, columns)


def assemble_kernel(in_ref, out_ref):
    out_ref[...] = jnp.zeros(out_ref.shape, BF)
    for a in range(8):
        for g in range(8):
            out_ref[a, g * GPAD : g * GPAD + GROUP, :] = in_ref[8 * a + g]


def assemble(arrived):
    vmem = pl.BlockSpec(memory_space=pltpu.VMEM)
    return pl.pallas_call(
        assemble_kernel,
        out_shape=jax.ShapeDtypeStruct((8, 8 * GPAD, 256), BF),
        in_specs=[vmem],
        out_specs=vmem,
        compiler_params=params(24),
        cost_estimate=pl.CostEstimate(flops=48 * 10**9, bytes_accessed=4 * 10**6, transcendentals=0),
        name="assemble_weight",
    )(arrived)


def receive_kernel(in_ref, weight_ref, rows_ref, part_ref, placed_scr, stack_scr):
    @pl.when(pl.program_id(0) == 0)
    def _():
        slots = in_ref.shape[0]
        numbers = in_ref[:, 4 * MAIN :].astype(F32).T[64:65]
        row = iota((256, slots), 0)
        wanted = (numbers == ((row >> 4) + 1).astype(F32)) & ((iota((256, slots), 1) & 15) == (row & 15))
        pick = jnp.where(wanted, 1.0, 0.0).astype(BF)
        for left in range(0, 4 * MAIN, MAIN):
            placed_scr[:, left : left + MAIN] = dot(pick, in_ref[:, left : left + MAIN]).astype(BF)
        rest = dot(pick, in_ref[:, 4 * MAIN :]).astype(BF)
        column = iota((MAIN, 8 * GPAD), 1)
        inside = (column & 63) < GROUP
        feature = (column >> 6) * GROUP + (column & 63)
        spread = jnp.where((feature == iota((MAIN, 8 * GPAD), 0)) & inside, 1.0, 0.0).astype(BF)
        row = iota((256, 256), 0)
        source = (row & 1) * 128 + (row >> 5) * 16 + ((row >> 1) & 15)
        order = jnp.where(iota((256, 256), 1) == source, 1.0, 0.0).astype(BF)
        lane = iota((128, 8 * GPAD), 0)
        for e in range(2):
            for u in range(2):
                k = 2 * e + u
                spread_rest = jnp.where(
                    (feature[0:128] == lane + (MAIN - 16 * k)) & inside[0:128] & (lane >= 16 * k) & (lane < 16 * k + 16),
                    1.0,
                    0.0,
                ).astype(BF)
                wide = (dot(placed_scr[:, k * MAIN : (k + 1) * MAIN], spread) + dot(rest, spread_rest)).astype(BF)
                stack_scr[0, u * 128 : (u + 1) * 128, :] = wide[0:128]
                stack_scr[1, u * 128 : (u + 1) * 128, :] = wide[128:256]
            for half in range(2):
                lower = e * 512 + half * 256
                rows_ref[lower : lower + 256, :] = dot(order, stack_scr[half]).astype(BF)

    for a in range(4):
        part_ref[a] = dot(rows_ref[...], weight_ref[a]).astype(BF)


def receive(arrived, weight):
    slots = arrived.shape[0]
    return pl.pallas_call(
        receive_kernel,
        grid=(2,),
        out_shape=(
            jax.ShapeDtypeStruct((1024, 512), BF),
            jax.ShapeDtypeStruct((8, 1024, 256), BF),
        ),
        in_specs=[
            pl.BlockSpec(memory_space=pltpu.VMEM),
            pl.BlockSpec((4, 8 * GPAD, 256), lambda a: (a, 0, 0)),
        ],
        out_specs=(
            pl.BlockSpec((1024, 512), lambda a: (0, 0)),
            pl.BlockSpec((4, 1024, 256), lambda a: (a, 0, 0)),
        ),
        scratch_shapes=[
            pltpu.VMEM((256, 4 * MAIN), BF),
            pltpu.VMEM((2, 256, 512), BF),
        ],
        compiler_params=params(60),
        name="receive_pieces",
    )(arrived, weight)


def forward_kernel(x_ref, p_ref, att_ref, a_ref, q_scr, vt_scr, a_scr):
    tail_row = iota((16, 128), 0) == 0
    q_scr[0:1024, :] = x_ref[0, 0, 0:1024, :]
    q_scr[1024:QPAD, :] = jnp.zeros((128, 128), BF)
    q_scr[1024:1040, :] = jnp.where(tail_row, x_ref[0, 0, 1024:1025, :].astype(F32), 0.0).astype(BF)
    key = x_ref[0, 1, 0:1024, :]
    key_tail = jnp.where(tail_row, x_ref[0, 1, 1024:1025, :].astype(F32), 0.0).astype(BF)
    vt_scr[...] = x_ref[0, 2, 0:1024, :].astype(F32).T.astype(BF)
    value_tail = jnp.where(tail_row, x_ref[0, 2, 1024:1025, :].astype(F32), 0.0).astype(BF)
    first = iota((16, QBLK), 0) == 0
    for j in range(QPAD // QBLK):
        span = slice(j * QBLK, (j + 1) * QBLK)
        query = q_scr[span, :]
        score = dot_last(key, query) * SCALE
        score_tail = (dot_last(key_tail, query) * SCALE)[0:1]
        top = jnp.maximum(jnp.max(score, axis=0, keepdims=True), score_tail)
        shifted = jnp.exp(score - top)
        shifted_tail = jnp.exp(score_tail - top)
        inverse = 1.0 / (jnp.sum(shifted, axis=0, keepdims=True) + shifted_tail)
        low = (shifted * inverse).astype(BF)
        low_tail = jnp.where(first, shifted_tail * inverse, 0.0).astype(BF)
        p_ref[0, 0:1024, span] = low
        p_ref[0, 1024:KPAD, span] = low_tail
        att = (dot(vt_scr[...], low) + dot_first(value_tail, low_tail)).T.astype(BF)
        att_ref[span, :] = att
        a_scr[span, :] = att.astype(F32)
    moved = a_scr[pl.ds(1, 1024), :].astype(BF)
    for i in range(NPIECE):
        for e in range(2):
            a_ref[512 * e + 32 * i : 512 * e + 32 * i + 32, :] = moved[64 * i + 32 * e : 64 * i + 32 * e + 32]


def forward(head_inputs):
    return pl.pallas_call(
        forward_kernel,
        grid=(2,),
        out_shape=(
            jax.ShapeDtypeStruct((2, KPAD, QPAD), BF),
            jax.ShapeDtypeStruct((QPAD, 256), BF),
            jax.ShapeDtypeStruct((PATCHES, 256), BF),
        ),
        in_specs=[pl.BlockSpec((1, 3, TT, HD), lambda h: (0, 0, 0, h))],
        out_specs=(
            pl.BlockSpec((1, KPAD, QPAD), lambda h: (h, 0, 0)),
            pl.BlockSpec((QPAD, HD), lambda h: (0, h)),
            pl.BlockSpec((PATCHES, HD), lambda h: (0, h)),
        ),
        scratch_shapes=[
            pltpu.VMEM((QPAD, HD), BF),
            pltpu.VMEM((HD, 1024), BF),
            pltpu.VMEM((QPAD, HD), F32),
        ],
        compiler_params=params(50),
        cost_estimate=pl.CostEstimate(flops=2 * 10**9, bytes_accessed=8 * 10**6, transcendentals=2 * 10**6),
        name="attend",
    )(head_inputs)


def backward_kernel(x_ref, p_ref, att_ref, o_ref, out_ref, q_scr, kt_scr, g_scr):
    tail_row = iota((16, 128), 0) == 0
    q_scr[0:1024, :] = x_ref[0, 0, 0:1024, :]
    q_scr[1024:QPAD, :] = jnp.zeros((128, 128), BF)
    q_scr[1024:1040, :] = jnp.where(tail_row, x_ref[0, 0, 1024:1025, :].astype(F32), 0.0).astype(BF)
    kt_scr[...] = x_ref[0, 1, 0:1024, :].astype(F32).T.astype(BF)
    key_tail = jnp.where(tail_row, x_ref[0, 1, 1024:1025, :].astype(F32), 0.0).astype(BF)
    value = x_ref[0, 2, 0:1024, :]
    value_tail = jnp.where(tail_row, x_ref[0, 2, 1024:1025, :].astype(F32), 0.0).astype(BF)
    g_scr[0:8, :] = jnp.zeros((8, HD), F32)
    g_scr[1024 : QPAD, :] = jnp.zeros((QPAD - 1024, HD), F32)
    for i in range(NPIECE):
        g_scr[pl.ds(1 + 64 * i, 32), :] = o_ref[32 * i : 32 * i + 32, :].astype(F32)
        g_scr[pl.ds(33 + 64 * i, 32), :] = o_ref[512 + 32 * i : 544 + 32 * i, :].astype(F32)
    query = q_scr[...]
    grad_wide = g_scr[...]
    grad = grad_wide.astype(BF)
    delta = jnp.sum((grad_wide * att_ref[...].astype(F32)).T, axis=0, keepdims=True)
    low_tail = p_ref[0, 1024:KPAD, :]
    inner_tail = (low_tail.astype(F32) * (dot_last(value_tail, grad) - delta)).astype(BF)
    dq = dot_first(key_tail, inner_tail)
    out_ref[0, 1, 1024:1025, :] = (dot(inner_tail, query) * SCALE).astype(BF)[0:1]
    out_ref[0, 2, 1024:1025, :] = dot(low_tail, grad).astype(BF)[0:1]
    low = p_ref[0, 0:1024, :]
    out_ref[0, 2, 0:1024, :] = dot(low, grad).astype(BF)
    inner = (low.astype(F32) * (dot_last(value, grad) - delta)).astype(BF)
    out_ref[0, 1, 0:1024, :] = (dot(inner, query) * SCALE).astype(BF)
    dq = dq + dot(kt_scr[...], inner)
    dq = (dq * SCALE).T.astype(BF)
    out_ref[0, 0, 0:1024, :] = dq[0:1024]
    out_ref[0, 0, 1024:1025, :] = dq[1024:1040][0:1]


def backward(head_inputs, probs, att, out_grad):
    return pl.pallas_call(
        backward_kernel,
        grid=(2,),
        out_shape=jax.ShapeDtypeStruct((1, 3, TT, 256), BF),
        in_specs=[
            pl.BlockSpec((1, 3, TT, HD), lambda h: (0, 0, 0, h)),
            pl.BlockSpec((1, KPAD, QPAD), lambda h: (h, 0, 0)),
            pl.BlockSpec((QPAD, HD), lambda h: (0, h)),
            pl.BlockSpec((PATCHES, HD), lambda h: (0, h)),
        ],
        out_specs=pl.BlockSpec((1, 3, TT, HD), lambda h: (0, 0, 0, h)),
        scratch_shapes=[
            pltpu.VMEM((QPAD, HD), BF),
            pltpu.VMEM((HD, 1024), BF),
            pltpu.VMEM((QPAD, HD), F32),
        ],
        compiler_params=params(60),
        name="attend_backward",
    )(head_inputs, probs, att, out_grad)


def weight_kernel(place_ref, r_ref, *refs):
    parts = refs[:8]
    keep_ref, send_ref, t_scr, sum_scr, part_scr, sems = refs[8:]
    copies = [pltpu.make_async_copy(parts[n], part_scr.at[n], sems.at[n]) for n in range(8)]
    for copy in copies:
        copy.start()
    t_scr[...] = r_ref[...].astype(F32).T.astype(BF)
    core = place_ref[0]
    for n in range(8):
        block = (place_ref[1] - n) & 7
        copies[n].wait()
        sum_scr[...] = dot(t_scr[...], part_scr[n])
        for x in range(4):
            mine = pl.multiple_of((2 * x + core) * GPAD, GPAD)
            other = pl.multiple_of((2 * x + 1 - core) * GPAD, GPAD)
            keep_ref[4 * block + x] = sum_scr[pl.ds(mine, GSEND), :]
            send_ref[4 * block + x] = sum_scr[pl.ds(other, GSEND), :].astype(BF)


def weight_parts(place, rows, gathered):
    vmem = pl.BlockSpec(memory_space=pltpu.VMEM)
    return pl.pallas_call(
        weight_kernel,
        out_shape=(
            jax.ShapeDtypeStruct((32, GSEND, 256), F32),
            jax.ShapeDtypeStruct((32, GSEND, 256), BF),
        ),
        in_specs=[pl.BlockSpec(memory_space=pltpu.SMEM), vmem] + [pl.BlockSpec(memory_space=pl.ANY)] * 8,
        out_specs=(vmem, vmem),
        scratch_shapes=[
            pltpu.VMEM((512, 1024), BF),
            pltpu.VMEM((512, 256), F32),
            pltpu.VMEM((8, PATCHES, 256), BF),
            pltpu.SemaphoreType.DMA((8,)),
        ],
        compiler_params=params(60),
        name="weight_parts",
    )(place, rows, *gathered)


def ring(count, step):
    return [(i, (i + step) % count) for i in range(count)]


def per_device(head_inputs, out_weight, sequence_gradient, slot_labels):
    peers = 64
    swap = [(z * 8 + y, y * 8 + z) for z in range(8) for y in range(8)]
    weight = lax.ppermute(out_weight, ("z", "y"), swap)
    place = jnp.stack([lax.axis_index(name).astype(jnp.int32) for name in ("c", "y")])
    outgoing = pack(slot_labels, sequence_gradient.transpose(0, 2, 1), peers)
    outgoing, head_inputs, weight = lax.optimization_barrier((outgoing, head_inputs, weight))
    weight = assemble(lax.all_gather(weight, SHARDS, axis=0))
    arrived = lax.all_to_all(outgoing, SHARDS, 0, 0, tiled=True)

    probs, att, parts = forward(head_inputs)
    back = [parts]
    for _ in range(4):
        back.append(lax.ppermute(back[-1], "y", ring(8, 1)))
    ahead = [parts]
    for _ in range(3):
        ahead.append(lax.ppermute(ahead[-1], "y", ring(8, -1)))
    arrived, *gathered = lax.optimization_barrier((arrived, *back, *ahead[:0:-1]))

    rows, part = receive(arrived.reshape(peers * PIECE, 4 * MAIN + 128), weight)
    out_grad = lax.psum_scatter(part, "y", scatter_dimension=0, tiled=True)[0]

    keep, send = weight_parts(place, rows, gathered)
    got = lax.ppermute(send, "c", [(0, 1), (1, 0)])
    both = (keep + got.astype(F32)).astype(BF)
    spread = lax.all_to_all(both, ("z", "x"), 0, 0, tiled=True)
    summed = jnp.sum(spread.astype(F32), axis=0)[:GROUP] * (1.0 / math.sqrt(65536))
    weight_gradient = lax.ppermute(summed, ("z", "y"), swap)

    head_gradient = backward(head_inputs, probs, att, out_grad)
    return head_gradient, weight_gradient


def solution(mesh):
    fine = Mesh(mesh.devices.reshape(8, 4, 2, 8), ("z", "x", "c", "y"))
    return jax.shard_map(
        per_device,
        mesh=fine,
        in_specs=(
            P(SHARDS, None, None, "y"),
            P(SHARDS, "y"),
            P(None, SHARDS, "y"),
            P(SHARDS, None),
        ),
        out_specs=(P(SHARDS, None, None, "y"), P(SHARDS, "y")),
        check_vma=False,
    )
```

```python
import functools
import math

import jax
import jax.numpy as jnp
from jax import lax
from jax.experimental import pallas as pl
from jax.experimental.pallas import tpu as pltpu
from jax.sharding import Mesh, PartitionSpec as P

HD = 128
TT = 1025
PATCHES = 1024
KPAD = 1040
QPAD = 1152
QBLK = 384
PIECE = 16
NPIECE = 16
MAIN = 384
GROUP = 50
GPAD = 64
GSEND = 56
BF = jnp.bfloat16
F32 = jnp.float32
SHARDS = ("z", "x", "c")
SCALE = HD ** (-0.5)


def dot(left, right):
    return jnp.dot(left, right, preferred_element_type=F32)


def dot_last(left, right):
    return lax.dot_general(left, right, (((1,), (1,)), ((), ())), preferred_element_type=F32)


def dot_first(left, right):
    return lax.dot_general(left, right, (((0,), (0,)), ((), ())), preferred_element_type=F32)


def iota(shape, axis):
    return lax.broadcasted_iota(jnp.int32, shape, axis)


def params(mebibytes):
    return pltpu.CompilerParams(vmem_limit_bytes=mebibytes * 1024 * 1024)


def pack_kernel(label_ref, x_ref, out_ref, rest_scr, goal_scr):
    positions = x_ref.shape[2]

    @pl.when(pl.program_id(0) == 0)
    def _():
        lane = iota((16, positions), 1)
        slot = lane >> 4
        goal = jnp.full((16, positions), -1, jnp.int32)
        for s in range(label_ref.shape[1]):
            goal = jnp.where(slot == s, label_ref[0, s], goal)
        number = jnp.where(goal >= 0, (goal & 15) + 1, 0)
        goal_scr[...] = jnp.where(goal >= 0, (goal >> 4) * 16 + (lane & 15), -1)
        rest_scr[...] = jnp.zeros(rest_scr.shape, BF)
        for k in range(4):
            rest_scr[16 * k : 16 * k + 16, :] = x_ref[k, MAIN : MAIN + 16, :]
        rest_scr[64:80, :] = jnp.where(iota((16, positions), 0) == 0, number, 0).astype(F32).astype(BF)

    step = out_ref.shape[0] * PIECE
    row = iota((step, positions), 0) + pl.program_id(0) * step
    pick = jnp.where(row == goal_scr[0:1, :], 1.0, 0.0).astype(BF)
    for k in range(0, 4, 2):
        moved = dot_last(pick, x_ref[k : k + 2, 0:MAIN, :].reshape(2 * MAIN, positions)).astype(BF)
        out_ref[:, :, k * MAIN : (k + 2) * MAIN] = moved.reshape(step // PIECE, PIECE, 2 * MAIN)
    moved = dot_last(pick, rest_scr[...]).astype(BF)
    out_ref[:, :, 4 * MAIN :] = moved.reshape(step // PIECE, PIECE, 128)


def pack(labels, columns, peers):
    features, positions = columns.shape[1:]
    return pl.pallas_call(
        pack_kernel,
        grid=(2,),
        out_shape=jax.ShapeDtypeStruct((peers, PIECE, 4 * MAIN + 128), BF),
        in_specs=[
            pl.BlockSpec(memory_space=pltpu.SMEM),
            pl.BlockSpec((4, features, positions), lambda r: (0, 0, 0)),
        ],
        out_specs=pl.BlockSpec((peers // 2, PIECE, 4 * MAIN + 128), lambda r: (r, 0, 0)),
        scratch_shapes=[pltpu.VMEM((128, positions), BF), pltpu.VMEM((16, positions), jnp.int32)],
        compiler_params=params(60),
        name="pack_pieces",
    )(labels, columns)


def assemble_kernel(in_ref, out_ref):
    out_ref[...] = jnp.zeros(out_ref.shape, BF)
    for a in range(8):
        for g in range(8):
            out_ref[a, g * GPAD : g * GPAD + GROUP, :] = in_ref[8 * a + g]


def assemble(arrived):
    vmem = pl.BlockSpec(memory_space=pltpu.VMEM)
    return pl.pallas_call(
        assemble_kernel,
        out_shape=jax.ShapeDtypeStruct((8, 8 * GPAD, 256), BF),
        in_specs=[vmem],
        out_specs=vmem,
        compiler_params=params(24),
        cost_estimate=pl.CostEstimate(flops=48 * 10**9, bytes_accessed=4 * 10**6, transcendentals=0),
        name="assemble_weight",
    )(arrived)


def receive_kernel(in_ref, weight_ref, rows_ref, part_ref, placed_scr, stack_scr):
    @pl.when(pl.program_id(0) == 0)
    def _():
        slots = in_ref.shape[0]
        numbers = in_ref[:, 4 * MAIN :].astype(F32).T[64:65]
        row = iota((256, slots), 0)
        wanted = (numbers == ((row >> 4) + 1).astype(F32)) & ((iota((256, slots), 1) & 15) == (row & 15))
        pick = jnp.where(wanted, 1.0, 0.0).astype(BF)
        for left in range(0, 4 * MAIN, MAIN):
            placed_scr[:, left : left + MAIN] = dot(pick, in_ref[:, left : left + MAIN]).astype(BF)
        rest = dot(pick, in_ref[:, 4 * MAIN :]).astype(BF)
        column = iota((MAIN, 8 * GPAD), 1)
        inside = (column & 63) < GROUP
        feature = (column >> 6) * GROUP + (column & 63)
        spread = jnp.where((feature == iota((MAIN, 8 * GPAD), 0)) & inside, 1.0, 0.0).astype(BF)
        row = iota((256, 256), 0)
        source = (row & 1) * 128 + (row >> 5) * 16 + ((row >> 1) & 15)
        order = jnp.where(iota((256, 256), 1) == source, 1.0, 0.0).astype(BF)
        lane = iota((128, 8 * GPAD), 0)
        for e in range(2):
            for u in range(2):
                k = 2 * e + u
                spread_rest = jnp.where(
                    (feature[0:128] == lane + (MAIN - 16 * k)) & inside[0:128] & (lane >= 16 * k) & (lane < 16 * k + 16),
                    1.0,
                    0.0,
                ).astype(BF)
                wide = (dot(placed_scr[:, k * MAIN : (k + 1) * MAIN], spread) + dot(rest, spread_rest)).astype(BF)
                stack_scr[0, u * 128 : (u + 1) * 128, :] = wide[0:128]
                stack_scr[1, u * 128 : (u + 1) * 128, :] = wide[128:256]
            for half in range(2):
                lower = e * 512 + half * 256
                rows_ref[lower : lower + 256, :] = dot(order, stack_scr[half]).astype(BF)

    for a in range(4):
        part_ref[a] = dot(rows_ref[...], weight_ref[a]).astype(BF)


def receive(arrived, weight):
    slots = arrived.shape[0]
    return pl.pallas_call(
        receive_kernel,
        grid=(2,),
        out_shape=(
            jax.ShapeDtypeStruct((1024, 512), BF),
            jax.ShapeDtypeStruct((8, 1024, 256), BF),
        ),
        in_specs=[
            pl.BlockSpec(memory_space=pltpu.VMEM),
            pl.BlockSpec((4, 8 * GPAD, 256), lambda a: (a, 0, 0)),
        ],
        out_specs=(
            pl.BlockSpec((1024, 512), lambda a: (0, 0)),
            pl.BlockSpec((4, 1024, 256), lambda a: (a, 0, 0)),
        ),
        scratch_shapes=[
            pltpu.VMEM((256, 4 * MAIN), BF),
            pltpu.VMEM((2, 256, 512), BF),
        ],
        compiler_params=params(60),
        name="receive_pieces",
    )(arrived, weight)


def forward_kernel(x_ref, p_ref, att_ref, a_ref, q_scr, vt_scr, a_scr):
    tail_row = iota((16, 128), 0) == 0
    q_scr[0:1024, :] = x_ref[0, 0, 0:1024, :]
    q_scr[1024:QPAD, :] = jnp.zeros((128, 128), BF)
    q_scr[1024:1040, :] = jnp.where(tail_row, x_ref[0, 0, 1024:1025, :].astype(F32), 0.0).astype(BF)
    key = x_ref[0, 1, 0:1024, :]
    key_tail = jnp.where(tail_row, x_ref[0, 1, 1024:1025, :].astype(F32), 0.0).astype(BF)
    vt_scr[...] = x_ref[0, 2, 0:1024, :].astype(F32).T.astype(BF)
    value_tail = jnp.where(tail_row, x_ref[0, 2, 1024:1025, :].astype(F32), 0.0).astype(BF)
    first = iota((16, QBLK), 0) == 0
    for j in range(QPAD // QBLK):
        span = slice(j * QBLK, (j + 1) * QBLK)
        query = q_scr[span, :]
        score = dot_last(key, query) * SCALE
        score_tail = (dot_last(key_tail, query) * SCALE)[0:1]
        top = jnp.maximum(jnp.max(score, axis=0, keepdims=True), score_tail)
        shifted = jnp.exp(score - top)
        shifted_tail = jnp.exp(score_tail - top)
        inverse = 1.0 / (jnp.sum(shifted, axis=0, keepdims=True) + shifted_tail)
        low = (shifted * inverse).astype(BF)
        low_tail = jnp.where(first, shifted_tail * inverse, 0.0).astype(BF)
        p_ref[0, 0:1024, span] = low
        p_ref[0, 1024:KPAD, span] = low_tail
        att = (dot(vt_scr[...], low) + dot_first(value_tail, low_tail)).T.astype(BF)
        att_ref[span, :] = att
        a_scr[span, :] = att.astype(F32)
    moved = a_scr[pl.ds(1, 1024), :].astype(BF)
    for i in range(NPIECE):
        for e in range(2):
            a_ref[512 * e + 32 * i : 512 * e + 32 * i + 32, :] = moved[64 * i + 32 * e : 64 * i + 32 * e + 32]


def forward(head_inputs):
    return pl.pallas_call(
        forward_kernel,
        grid=(2,),
        out_shape=(
            jax.ShapeDtypeStruct((2, KPAD, QPAD), BF),
            jax.ShapeDtypeStruct((QPAD, 256), BF),
            jax.ShapeDtypeStruct((PATCHES, 256), BF),
        ),
        in_specs=[pl.BlockSpec((1, 3, TT, HD), lambda h: (0, 0, 0, h))],
        out_specs=(
            pl.BlockSpec((1, KPAD, QPAD), lambda h: (h, 0, 0)),
            pl.BlockSpec((QPAD, HD), lambda h: (0, h)),
            pl.BlockSpec((PATCHES, HD), lambda h: (0, h)),
        ),
        scratch_shapes=[
            pltpu.VMEM((QPAD, HD), BF),
            pltpu.VMEM((HD, 1024), BF),
            pltpu.VMEM((QPAD, HD), F32),
        ],
        compiler_params=params(50),
        cost_estimate=pl.CostEstimate(flops=2 * 10**9, bytes_accessed=8 * 10**6, transcendentals=2 * 10**6),
        name="attend",
    )(head_inputs)


def backward_kernel(x_ref, p_ref, att_ref, o_ref, out_ref, q_scr, kt_scr, g_scr):
    tail_row = iota((16, 128), 0) == 0
    q_scr[0:1024, :] = x_ref[0, 0, 0:1024, :]
    q_scr[1024:QPAD, :] = jnp.zeros((128, 128), BF)
    q_scr[1024:1040, :] = jnp.where(tail_row, x_ref[0, 0, 1024:1025, :].astype(F32), 0.0).astype(BF)
    kt_scr[...] = x_ref[0, 1, 0:1024, :].astype(F32).T.astype(BF)
    key_tail = jnp.where(tail_row, x_ref[0, 1, 1024:1025, :].astype(F32), 0.0).astype(BF)
    value = x_ref[0, 2, 0:1024, :]
    value_tail = jnp.where(tail_row, x_ref[0, 2, 1024:1025, :].astype(F32), 0.0).astype(BF)
    g_scr[0:8, :] = jnp.zeros((8, HD), F32)
    g_scr[1024 : QPAD, :] = jnp.zeros((QPAD - 1024, HD), F32)
    for i in range(NPIECE):
        g_scr[pl.ds(1 + 64 * i, 32), :] = o_ref[32 * i : 32 * i + 32, :].astype(F32)
        g_scr[pl.ds(33 + 64 * i, 32), :] = o_ref[512 + 32 * i : 544 + 32 * i, :].astype(F32)
    query = q_scr[...]
    grad_wide = g_scr[...]
    grad = grad_wide.astype(BF)
    delta = jnp.sum((grad_wide * att_ref[...].astype(F32)).T, axis=0, keepdims=True)
    low_tail = p_ref[0, 1024:KPAD, :]
    inner_tail = (low_tail.astype(F32) * (dot_last(value_tail, grad) - delta)).astype(BF)
    dq = dot_first(key_tail, inner_tail)
    out_ref[0, 1, 1024:1025, :] = (dot(inner_tail, query) * SCALE).astype(BF)[0:1]
    out_ref[0, 2, 1024:1025, :] = dot(low_tail, grad).astype(BF)[0:1]
    low = p_ref[0, 0:1024, :]
    out_ref[0, 2, 0:1024, :] = dot(low, grad).astype(BF)
    inner = (low.astype(F32) * (dot_last(value, grad) - delta)).astype(BF)
    out_ref[0, 1, 0:1024, :] = (dot(inner, query) * SCALE).astype(BF)
    dq = dq + dot(kt_scr[...], inner)
    dq = (dq * SCALE).T.astype(BF)
    out_ref[0, 0, 0:1024, :] = dq[0:1024]
    out_ref[0, 0, 1024:1025, :] = dq[1024:1040][0:1]


def backward(head_inputs, probs, att, out_grad):
    return pl.pallas_call(
        backward_kernel,
        grid=(2,),
        out_shape=jax.ShapeDtypeStruct((1, 3, TT, 256), BF),
        in_specs=[
            pl.BlockSpec((1, 3, TT, HD), lambda h: (0, 0, 0, h)),
            pl.BlockSpec((1, KPAD, QPAD), lambda h: (h, 0, 0)),
            pl.BlockSpec((QPAD, HD), lambda h: (0, h)),
            pl.BlockSpec((PATCHES, HD), lambda h: (0, h)),
        ],
        out_specs=pl.BlockSpec((1, 3, TT, HD), lambda h: (0, 0, 0, h)),
        scratch_shapes=[
            pltpu.VMEM((QPAD, HD), BF),
            pltpu.VMEM((HD, 1024), BF),
            pltpu.VMEM((QPAD, HD), F32),
        ],
        compiler_params=params(60),
        name="attend_backward",
    )(head_inputs, probs, att, out_grad)


def weight_kernel(place_ref, r_ref, *refs):
    parts = refs[:8]
    keep_ref, send_ref, t_scr, sum_scr, part_scr, sems = refs[8:]
    copies = [pltpu.make_async_copy(parts[n], part_scr.at[n], sems.at[n]) for n in range(8)]
    for copy in copies:
        copy.start()
    t_scr[...] = r_ref[...].astype(F32).T.astype(BF)
    core = place_ref[0]
    for n in range(8):
        block = (place_ref[1] - n) & 7
        copies[n].wait()
        sum_scr[...] = dot(t_scr[...], part_scr[n])
        for x in range(4):
            mine = pl.multiple_of((2 * x + core) * GPAD, GPAD)
            other = pl.multiple_of((2 * x + 1 - core) * GPAD, GPAD)
            keep_ref[4 * block + x] = sum_scr[pl.ds(mine, GSEND), :]
            send_ref[4 * block + x] = sum_scr[pl.ds(other, GSEND), :].astype(BF)


def weight_parts(place, rows, gathered):
    vmem = pl.BlockSpec(memory_space=pltpu.VMEM)
    return pl.pallas_call(
        weight_kernel,
        out_shape=(
            jax.ShapeDtypeStruct((32, GSEND, 256), F32),
            jax.ShapeDtypeStruct((32, GSEND, 256), BF),
        ),
        in_specs=[pl.BlockSpec(memory_space=pltpu.SMEM), vmem] + [pl.BlockSpec(memory_space=pl.ANY)] * 8,
        out_specs=(vmem, vmem),
        scratch_shapes=[
            pltpu.VMEM((512, 1024), BF),
            pltpu.VMEM((512, 256), F32),
            pltpu.VMEM((8, PATCHES, 256), BF),
            pltpu.SemaphoreType.DMA((8,)),
        ],
        compiler_params=params(60),
        name="weight_parts",
    )(place, rows, *gathered)


def ring(count, step):
    return [(i, (i + step) % count) for i in range(count)]


def per_device(head_inputs, out_weight, sequence_gradient, slot_labels):
    peers = 64
    swap = [(z * 8 + y, y * 8 + z) for z in range(8) for y in range(8)]
    weight = lax.ppermute(out_weight, ("z", "y"), swap)
    place = jnp.stack([lax.axis_index(name).astype(jnp.int32) for name in ("c", "y")])
    outgoing = pack(slot_labels, sequence_gradient.transpose(0, 2, 1), peers)
    outgoing, head_inputs, weight = lax.optimization_barrier((outgoing, head_inputs, weight))
    weight = assemble(lax.all_gather(weight, SHARDS, axis=0))
    arrived = lax.all_to_all(outgoing, SHARDS, 0, 0, tiled=True)

    probs, att, parts = forward(head_inputs)
    back = [parts]
    for _ in range(4):
        back.append(lax.ppermute(back[-1], "y", ring(8, 1)))
    ahead = [parts]
    for _ in range(3):
        ahead.append(lax.ppermute(ahead[-1], "y", ring(8, -1)))
    arrived, *gathered = lax.optimization_barrier((arrived, *back, *ahead[:0:-1]))

    rows, part = receive(arrived.reshape(peers * PIECE, 4 * MAIN + 128), weight)
    out_grad = lax.psum_scatter(part, "y", scatter_dimension=0, tiled=True)[0]

    keep, send = weight_parts(place, rows, gathered)
    got = lax.ppermute(send, "c", [(0, 1), (1, 0)])
    both = (keep + got.astype(F32)).astype(BF)
    spread = lax.all_to_all(both, ("z", "x"), 0, 0, tiled=True)
    summed = jnp.sum(spread.astype(F32), axis=0)[:GROUP] * (1.0 / math.sqrt(65536))
    weight_gradient = lax.ppermute(summed, ("z", "y"), swap)

    head_gradient = backward(head_inputs, probs, att, out_grad)
    return lax.optimization_barrier((head_gradient, weight_gradient))


def solution(mesh):
    fine = Mesh(mesh.devices.reshape(8, 4, 2, 8), ("z", "x", "c", "y"))
    return jax.shard_map(
        per_device,
        mesh=fine,
        in_specs=(
            P(SHARDS, None, None, "y"),
            P(SHARDS, "y"),
            P(None, SHARDS, "y"),
            P(SHARDS, None),
        ),
        out_specs=(P(SHARDS, None, None, "y"), P(SHARDS, "y")),
        check_vma=False,
    )
```

```python
import functools
import math

import jax
import jax.numpy as jnp
from jax import lax
from jax.experimental import pallas as pl
from jax.experimental.pallas import tpu as pltpu
from jax.sharding import Mesh, PartitionSpec as P

HD = 128
TT = 1025
PATCHES = 1024
KPAD = 1040
QPAD = 1152
QBLK = 384
PIECE = 16
NPIECE = 16
MAIN = 384
GROUP = 50
GPAD = 64
GSEND = 56
BF = jnp.bfloat16
F32 = jnp.float32
SHARDS = ("z", "x", "c")
SCALE = HD ** (-0.5)


def dot(left, right):
    return jnp.dot(left, right, preferred_element_type=F32)


def dot_last(left, right):
    return lax.dot_general(left, right, (((1,), (1,)), ((), ())), preferred_element_type=F32)


def dot_first(left, right):
    return lax.dot_general(left, right, (((0,), (0,)), ((), ())), preferred_element_type=F32)


def iota(shape, axis):
    return lax.broadcasted_iota(jnp.int32, shape, axis)


def params(mebibytes):
    return pltpu.CompilerParams(vmem_limit_bytes=mebibytes * 1024 * 1024)


def pack_kernel(label_ref, x_ref, out_ref, rest_scr, goal_scr):
    positions = x_ref.shape[2]

    @pl.when(pl.program_id(0) == 0)
    def _():
        lane = iota((16, positions), 1)
        slot = lane >> 4
        goal = jnp.full((16, positions), -1, jnp.int32)
        for s in range(label_ref.shape[1]):
            goal = jnp.where(slot == s, label_ref[0, s], goal)
        number = jnp.where(goal >= 0, (goal & 15) + 1, 0)
        goal_scr[...] = jnp.where(goal >= 0, (goal >> 4) * 16 + (lane & 15), -1)
        rest_scr[...] = jnp.zeros(rest_scr.shape, BF)
        for k in range(4):
            rest_scr[16 * k : 16 * k + 16, :] = x_ref[k, MAIN : MAIN + 16, :]
        rest_scr[64:80, :] = jnp.where(iota((16, positions), 0) == 0, number, 0).astype(F32).astype(BF)

    step = out_ref.shape[0] * PIECE
    row = iota((step, positions), 0) + pl.program_id(0) * step
    pick = jnp.where(row == goal_scr[0:1, :], 1.0, 0.0).astype(BF)
    for k in range(0, 4, 2):
        moved = dot_last(pick, x_ref[k : k + 2, 0:MAIN, :].reshape(2 * MAIN, positions)).astype(BF)
        out_ref[:, :, k * MAIN : (k + 2) * MAIN] = moved.reshape(step // PIECE, PIECE, 2 * MAIN)
    moved = dot_last(pick, rest_scr[...]).astype(BF)
    out_ref[:, :, 4 * MAIN :] = moved.reshape(step // PIECE, PIECE, 128)


def pack(labels, columns, peers):
    features, positions = columns.shape[1:]
    return pl.pallas_call(
        pack_kernel,
        grid=(2,),
        out_shape=jax.ShapeDtypeStruct((peers, PIECE, 4 * MAIN + 128), BF),
        in_specs=[
            pl.BlockSpec(memory_space=pltpu.SMEM),
            pl.BlockSpec((4, features, positions), lambda r: (0, 0, 0)),
        ],
        out_specs=pl.BlockSpec((peers // 2, PIECE, 4 * MAIN + 128), lambda r: (r, 0, 0)),
        scratch_shapes=[pltpu.VMEM((128, positions), BF), pltpu.VMEM((16, positions), jnp.int32)],
        compiler_params=params(60),
        name="pack_pieces",
    )(labels, columns)


def assemble_kernel(in_ref, out_ref):
    out_ref[...] = jnp.zeros(out_ref.shape, BF)
    for a in range(8):
        for g in range(8):
            out_ref[a, g * GPAD : g * GPAD + GROUP, :] = in_ref[8 * a + g]


def assemble(arrived):
    vmem = pl.BlockSpec(memory_space=pltpu.VMEM)
    return pl.pallas_call(
        assemble_kernel,
        out_shape=jax.ShapeDtypeStruct((8, 8 * GPAD, 256), BF),
        in_specs=[vmem],
        out_specs=vmem,
        compiler_params=params(60),
        cost_estimate=pl.CostEstimate(flops=48 * 10**9, bytes_accessed=4 * 10**6, transcendentals=0),
        name="assemble_weight",
    )(arrived)


def receive_kernel(in_ref, weight_ref, rows_ref, part_ref, placed_scr, stack_scr):
    @pl.when(pl.program_id(0) == 0)
    def _():
        slots = in_ref.shape[0]
        numbers = in_ref[:, 4 * MAIN :].astype(F32).T[64:65]
        row = iota((256, slots), 0)
        wanted = (numbers == ((row >> 4) + 1).astype(F32)) & ((iota((256, slots), 1) & 15) == (row & 15))
        pick = jnp.where(wanted, 1.0, 0.0).astype(BF)
        for left in range(0, 4 * MAIN, MAIN):
            placed_scr[:, left : left + MAIN] = dot(pick, in_ref[:, left : left + MAIN]).astype(BF)
        rest = dot(pick, in_ref[:, 4 * MAIN :]).astype(BF)
        column = iota((MAIN, 8 * GPAD), 1)
        inside = (column & 63) < GROUP
        feature = (column >> 6) * GROUP + (column & 63)
        spread = jnp.where((feature == iota((MAIN, 8 * GPAD), 0)) & inside, 1.0, 0.0).astype(BF)
        row = iota((256, 256), 0)
        source = (row & 1) * 128 + (row >> 5) * 16 + ((row >> 1) & 15)
        order = jnp.where(iota((256, 256), 1) == source, 1.0, 0.0).astype(BF)
        lane = iota((128, 8 * GPAD), 0)
        for e in range(2):
            for u in range(2):
                k = 2 * e + u
                spread_rest = jnp.where(
                    (feature[0:128] == lane + (MAIN - 16 * k)) & inside[0:128] & (lane >= 16 * k) & (lane < 16 * k + 16),
                    1.0,
                    0.0,
                ).astype(BF)
                wide = (dot(placed_scr[:, k * MAIN : (k + 1) * MAIN], spread) + dot(rest, spread_rest)).astype(BF)
                stack_scr[0, u * 128 : (u + 1) * 128, :] = wide[0:128]
                stack_scr[1, u * 128 : (u + 1) * 128, :] = wide[128:256]
            for half in range(2):
                lower = e * 512 + half * 256
                rows_ref[lower : lower + 256, :] = dot(order, stack_scr[half]).astype(BF)

    for a in range(4):
        part_ref[a] = dot(rows_ref[...], weight_ref[a]).astype(BF)


def receive(arrived, weight):
    slots = arrived.shape[0]
    return pl.pallas_call(
        receive_kernel,
        grid=(2,),
        out_shape=(
            jax.ShapeDtypeStruct((1024, 512), BF),
            jax.ShapeDtypeStruct((8, 1024, 256), BF),
        ),
        in_specs=[
            pl.BlockSpec(memory_space=pltpu.VMEM),
            pl.BlockSpec((4, 8 * GPAD, 256), lambda a: (a, 0, 0)),
        ],
        out_specs=(
            pl.BlockSpec((1024, 512), lambda a: (0, 0)),
            pl.BlockSpec((4, 1024, 256), lambda a: (a, 0, 0)),
        ),
        scratch_shapes=[
            pltpu.VMEM((256, 4 * MAIN), BF),
            pltpu.VMEM((2, 256, 512), BF),
        ],
        compiler_params=params(60),
        name="receive_pieces",
    )(arrived, weight)


def forward_kernel(x_ref, p_ref, att_ref, a_ref, q_scr, vt_scr, a_scr):
    tail_row = iota((16, 128), 0) == 0
    q_scr[0:1024, :] = x_ref[0, 0, 0:1024, :]
    q_scr[1024:QPAD, :] = jnp.zeros((128, 128), BF)
    q_scr[1024:1040, :] = jnp.where(tail_row, x_ref[0, 0, 1024:1025, :].astype(F32), 0.0).astype(BF)
    key = x_ref[0, 1, 0:1024, :]
    key_tail = jnp.where(tail_row, x_ref[0, 1, 1024:1025, :].astype(F32), 0.0).astype(BF)
    vt_scr[...] = x_ref[0, 2, 0:1024, :].astype(F32).T.astype(BF)
    value_tail = jnp.where(tail_row, x_ref[0, 2, 1024:1025, :].astype(F32), 0.0).astype(BF)
    first = iota((16, QBLK), 0) == 0
    for j in range(QPAD // QBLK):
        span = slice(j * QBLK, (j + 1) * QBLK)
        query = q_scr[span, :]
        score = dot_last(key, query) * SCALE
        score_tail = (dot_last(key_tail, query) * SCALE)[0:1]
        top = jnp.maximum(jnp.max(score, axis=0, keepdims=True), score_tail)
        shifted = jnp.exp(score - top)
        shifted_tail = jnp.exp(score_tail - top)
        inverse = 1.0 / (jnp.sum(shifted, axis=0, keepdims=True) + shifted_tail)
        low = (shifted * inverse).astype(BF)
        low_tail = jnp.where(first, shifted_tail * inverse, 0.0).astype(BF)
        p_ref[0, 0:1024, span] = low
        p_ref[0, 1024:KPAD, span] = low_tail
        att = (dot(vt_scr[...], low) + dot_first(value_tail, low_tail)).T.astype(BF)
        att_ref[span, :] = att
        a_scr[span, :] = att.astype(F32)
    moved = a_scr[pl.ds(1, 1024), :].astype(BF)
    for i in range(NPIECE):
        for e in range(2):
            a_ref[512 * e + 32 * i : 512 * e + 32 * i + 32, :] = moved[64 * i + 32 * e : 64 * i + 32 * e + 32]


def forward(head_inputs):
    return pl.pallas_call(
        forward_kernel,
        grid=(2,),
        out_shape=(
            jax.ShapeDtypeStruct((2, KPAD, QPAD), BF),
            jax.ShapeDtypeStruct((QPAD, 256), BF),
            jax.ShapeDtypeStruct((PATCHES, 256), BF),
        ),
        in_specs=[pl.BlockSpec((1, 3, TT, HD), lambda h: (0, 0, 0, h))],
        out_specs=(
            pl.BlockSpec((1, KPAD, QPAD), lambda h: (h, 0, 0)),
            pl.BlockSpec((QPAD, HD), lambda h: (0, h)),
            pl.BlockSpec((PATCHES, HD), lambda h: (0, h)),
        ),
        scratch_shapes=[
            pltpu.VMEM((QPAD, HD), BF),
            pltpu.VMEM((HD, 1024), BF),
            pltpu.VMEM((QPAD, HD), F32),
        ],
        compiler_params=params(50),
        cost_estimate=pl.CostEstimate(flops=2 * 10**9, bytes_accessed=8 * 10**6, transcendentals=2 * 10**6),
        name="attend",
    )(head_inputs)


def backward_kernel(x_ref, p_ref, att_ref, o_ref, out_ref, q_scr, kt_scr, g_scr):
    tail_row = iota((16, 128), 0) == 0
    q_scr[0:1024, :] = x_ref[0, 0, 0:1024, :]
    q_scr[1024:QPAD, :] = jnp.zeros((128, 128), BF)
    q_scr[1024:1040, :] = jnp.where(tail_row, x_ref[0, 0, 1024:1025, :].astype(F32), 0.0).astype(BF)
    kt_scr[...] = x_ref[0, 1, 0:1024, :].astype(F32).T.astype(BF)
    key_tail = jnp.where(tail_row, x_ref[0, 1, 1024:1025, :].astype(F32), 0.0).astype(BF)
    value = x_ref[0, 2, 0:1024, :]
    value_tail = jnp.where(tail_row, x_ref[0, 2, 1024:1025, :].astype(F32), 0.0).astype(BF)
    g_scr[0:8, :] = jnp.zeros((8, HD), F32)
    g_scr[1024 : QPAD, :] = jnp.zeros((QPAD - 1024, HD), F32)
    for i in range(NPIECE):
        g_scr[pl.ds(1 + 64 * i, 32), :] = o_ref[32 * i : 32 * i + 32, :].astype(F32)
        g_scr[pl.ds(33 + 64 * i, 32), :] = o_ref[512 + 32 * i : 544 + 32 * i, :].astype(F32)
    query = q_scr[...]
    grad_wide = g_scr[...]
    grad = grad_wide.astype(BF)
    delta = jnp.sum((grad_wide * att_ref[...].astype(F32)).T, axis=0, keepdims=True)
    low_tail = p_ref[0, 1024:KPAD, :]
    inner_tail = (low_tail.astype(F32) * (dot_last(value_tail, grad) - delta)).astype(BF)
    dq = dot_first(key_tail, inner_tail)
    out_ref[0, 1, 1024:1025, :] = (dot(inner_tail, query) * SCALE).astype(BF)[0:1]
    out_ref[0, 2, 1024:1025, :] = dot(low_tail, grad).astype(BF)[0:1]
    low = p_ref[0, 0:1024, :]
    out_ref[0, 2, 0:1024, :] = dot(low, grad).astype(BF)
    inner = (low.astype(F32) * (dot_last(value, grad) - delta)).astype(BF)
    out_ref[0, 1, 0:1024, :] = (dot(inner, query) * SCALE).astype(BF)
    dq = dq + dot(kt_scr[...], inner)
    dq = (dq * SCALE).T.astype(BF)
    out_ref[0, 0, 0:1024, :] = dq[0:1024]
    out_ref[0, 0, 1024:1025, :] = dq[1024:1040][0:1]


def backward(head_inputs, probs, att, out_grad):
    return pl.pallas_call(
        backward_kernel,
        grid=(2,),
        out_shape=jax.ShapeDtypeStruct((1, 3, TT, 256), BF),
        in_specs=[
            pl.BlockSpec((1, 3, TT, HD), lambda h: (0, 0, 0, h)),
            pl.BlockSpec((1, KPAD, QPAD), lambda h: (h, 0, 0)),
            pl.BlockSpec((QPAD, HD), lambda h: (0, h)),
            pl.BlockSpec((PATCHES, HD), lambda h: (0, h)),
        ],
        out_specs=pl.BlockSpec((1, 3, TT, HD), lambda h: (0, 0, 0, h)),
        scratch_shapes=[
            pltpu.VMEM((QPAD, HD), BF),
            pltpu.VMEM((HD, 1024), BF),
            pltpu.VMEM((QPAD, HD), F32),
        ],
        compiler_params=params(60),
        name="attend_backward",
    )(head_inputs, probs, att, out_grad)


def weight_kernel(place_ref, r_ref, *refs):
    parts = refs[:8]
    keep_ref, send_ref, t_scr, sum_scr, part_scr, sems = refs[8:]
    copies = [pltpu.make_async_copy(parts[n], part_scr.at[n], sems.at[n]) for n in range(8)]
    for copy in copies:
        copy.start()
    t_scr[...] = r_ref[...].astype(F32).T.astype(BF)
    core = place_ref[0]
    for n in range(8):
        block = (place_ref[1] - n) & 7
        copies[n].wait()
        sum_scr[...] = dot(t_scr[...], part_scr[n])
        for x in range(4):
            mine = pl.multiple_of((2 * x + core) * GPAD, GPAD)
            other = pl.multiple_of((2 * x + 1 - core) * GPAD, GPAD)
            keep_ref[4 * block + x] = sum_scr[pl.ds(mine, GSEND), :]
            send_ref[4 * block + x] = sum_scr[pl.ds(other, GSEND), :].astype(BF)


def weight_parts(place, rows, gathered):
    vmem = pl.BlockSpec(memory_space=pltpu.VMEM)
    return pl.pallas_call(
        weight_kernel,
        out_shape=(
            jax.ShapeDtypeStruct((32, GSEND, 256), F32),
            jax.ShapeDtypeStruct((32, GSEND, 256), BF),
        ),
        in_specs=[pl.BlockSpec(memory_space=pltpu.SMEM), vmem] + [pl.BlockSpec(memory_space=pl.ANY)] * 8,
        out_specs=(vmem, vmem),
        scratch_shapes=[
            pltpu.VMEM((512, 1024), BF),
            pltpu.VMEM((512, 256), F32),
            pltpu.VMEM((8, PATCHES, 256), BF),
            pltpu.SemaphoreType.DMA((8,)),
        ],
        compiler_params=params(60),
        name="weight_parts",
    )(place, rows, *gathered)


def ring(count, step):
    return [(i, (i + step) % count) for i in range(count)]


def per_device(head_inputs, out_weight, sequence_gradient, slot_labels):
    peers = 64
    swap = [(z * 8 + y, y * 8 + z) for z in range(8) for y in range(8)]
    weight = lax.ppermute(out_weight, ("z", "y"), swap)
    place = jnp.stack([lax.axis_index(name).astype(jnp.int32) for name in ("c", "y")])
    outgoing = pack(slot_labels, sequence_gradient.transpose(0, 2, 1), peers)
    outgoing, head_inputs, weight = lax.optimization_barrier((outgoing, head_inputs, weight))
    weight = assemble(lax.all_gather(weight, SHARDS, axis=0))
    arrived = lax.all_to_all(outgoing, SHARDS, 0, 0, tiled=True)

    probs, att, parts = forward(head_inputs)
    back = [parts]
    for _ in range(4):
        back.append(lax.ppermute(back[-1], "y", ring(8, 1)))
    ahead = [parts]
    for _ in range(3):
        ahead.append(lax.ppermute(ahead[-1], "y", ring(8, -1)))
    arrived, *gathered = lax.optimization_barrier((arrived, *back, *ahead[:0:-1]))

    rows, part = receive(arrived.reshape(peers * PIECE, 4 * MAIN + 128), weight)
    out_grad = lax.psum_scatter(part, "y", scatter_dimension=0, tiled=True)[0]

    keep, send = weight_parts(place, rows, gathered)
    got = lax.ppermute(send, "c", [(0, 1), (1, 0)])
    both = (keep + got.astype(F32)).astype(BF)
    spread = lax.all_to_all(both, ("z", "x"), 0, 0, tiled=True)
    summed = jnp.sum(spread.astype(F32), axis=0)[:GROUP] * (1.0 / math.sqrt(65536))
    weight_gradient = lax.ppermute(summed, ("z", "y"), swap)

    head_gradient = backward(head_inputs, probs, att, out_grad)
    return lax.optimization_barrier((head_gradient, weight_gradient))


def solution(mesh):
    fine = Mesh(mesh.devices.reshape(8, 4, 2, 8), ("z", "x", "c", "y"))
    return jax.shard_map(
        per_device,
        mesh=fine,
        in_specs=(
            P(SHARDS, None, None, "y"),
            P(SHARDS, "y"),
            P(None, SHARDS, "y"),
            P(SHARDS, None),
        ),
        out_specs=(P(SHARDS, None, None, "y"), P(SHARDS, "y")),
        check_vma=False,
    )
```
